256 devices in a mesh: lat: 16 (over x, z_lo, core), trc: 16 (over y, z_hi).
Axes of the slice: x: 4, y: 4, z: 8 (z_hi: 4, z_lo: 2; z = z_hi * 2 + z_lo), core: 2. Of those that a mesh axis runs over, the one named last changes fastest.
Arguments:
- tracers: float32 [128, 4, 128, 512], P('trc', None, 'lat'), may hold values from -6 to 6
- transports: float32 [2, 16, 3, 4, 128, 512], P(None, 'trc', None, None, 'lat'), may hold values from -0.1 to 0.1
- thickness: float32 [2, 16, 4, 128, 512], P(None, 'trc', None, 'lat'), may hold values from 1 to 2
- owner: int32 [2], replicated, may hold values from 0 to 15
- land_sea: int32 [128, 512], P('lat'), may hold values 0 or 1
- pairs: int32 [128], P('trc'), may hold values from 0 to 127, as said below
- rates: float32 [128], P('trc'), may hold values from 0.05 to 0.5
Outputs:
- result: float32 [128, 4, 128, 512], P('trc', None, 'lat')
The draws below stay inside these ranges and needn't reach their ends.
Inputs may be any that keep to these rules, and one draw needn't show every extreme that they name: owner[s] is the index along trc whose record slot holds step s's transports and thicknesses. pairs[i] is a tracer other than i in the same group of 8 consecutive tracers as i, and every tracer is some tracer's partner.
All inputs are finite; a program needn't handle non-finite values. No bound on the sum of `land_sea` on one device may be relied on, other than what follows from the above.
Results may differ from the reference program's by a relative error of at most 0.0003.
Values sent between devices are 32-bit elements; how exact they have to be, the bound alone decides.
A program may use at most 64 MiB of HBM per device.

```python
import math
import jax
import jax.numpy as jnp
from jax import lax

TRC_DEV = 8
LEV = 4
LON = 512
STEPS = 2
NLAT = 128
TRACERS = 128
ARCHIVES = 16
N_TRC = 16


def draw_pairs(key, part):
    groups = TRACERS // TRC_DEV
    keys = jax.random.split(key, groups)

    def one_order(single_key):
        order = jax.random.permutation(single_key, TRC_DEV).astype(jnp.int32)
        following = jnp.roll(order, -1)
        return jnp.zeros((TRC_DEV,), jnp.int32).at[order].set(following)
    partner = jax.vmap(one_order)(keys)
    base = (jnp.arange(groups, dtype=jnp.int32) * TRC_DEV)[:, None]
    return (partner + base).reshape(TRACERS).astype(jnp.int32)


def set_ends(values, key, smallest, top_value):
    place = [jax.random.randint(jax.random.fold_in(key, axis), (), 0, length) for axis, length in enumerate(values.shape)]
    main_axis = values.shape.index(max(values.shape))
    beside = place[:main_axis] + [(place[main_axis] + 1) % values.shape[main_axis]] + place[main_axis + 1:]
    return values.at[tuple(place)].set(smallest).at[tuple(beside)].set(top_value)


def levels(key, extent, cuts, smallest, largest):
    level = 1.0
    for axis_at, blocks in cuts:
        steps = jax.random.uniform(jax.random.fold_in(jax.random.fold_in(key, 6), axis_at), (blocks,), jnp.float32, smallest / len(cuts), largest / len(cuts))
        level = level * jnp.repeat(jnp.exp(steps), extent[axis_at] // blocks).reshape((-1,) + (1,) * (len(extent) - 1 - axis_at))
    return level


def centred(rng, dims, scale, reach, shards=(), kind=jnp.bfloat16):
    values = scale * jax.random.normal(rng, dims, jnp.float32)
    if shards:
        values = values * levels(rng, dims, shards, -0.22, 0.18)
    return jnp.clip(values, -reach, reach).astype(kind)


def setup_inputs(seed: int = 0) -> dict:
    key_list = jax.random.split(jax.random.key(seed), 8)
    tracers = centred(key_list[0], (TRACERS, LEV, NLAT, LON), 1.0, 6.0, ((0, 16), (2, 16)), jnp.float32)
    transports = jnp.clip(jax.random.uniform(key_list[1], (STEPS, ARCHIVES, 3, LEV, NLAT, LON), jnp.float32, -0.1, 0.1) * levels(key_list[1], (STEPS, ARCHIVES, 3, LEV, NLAT, LON), ((1, 16), (4, 16)), -0.4, 0.0), -0.1, 0.1)
    thickness = jnp.clip(1.0 + 1.0 * jax.random.uniform(key_list[2], (STEPS, ARCHIVES, LEV, NLAT, LON), jnp.float32) ** levels(key_list[2], (STEPS, ARCHIVES, LEV, NLAT, LON), ((1, 16), (3, 16)), -0.2, 0.2), 1.0, 2.0)
    owner = jax.random.randint(key_list[3], (STEPS,), 0, N_TRC).astype(jnp.int32)
    land_sea = set_ends((jax.random.randint(key_list[4], (NLAT, LON), 0, 10) < 9).astype(jnp.int32), jax.random.fold_in(key_list[4], 1), 0, 1)
    pairs = draw_pairs(jax.random.fold_in(key_list[7], 71), 0)
    rates = jnp.clip(jnp.exp(math.log(0.5) - 2.3025851 * jax.random.uniform(key_list[6], (TRACERS,), jnp.float32) ** levels(key_list[6], (TRACERS,), ((0, 16),), -0.2, 0.2)), 0.05, 0.5)
    return {"tracers": tracers, "transports": transports, "thickness": thickness, "owner": owner, "land_sea": land_sea, "pairs": pairs, "rates": rates}


def cut_along(array, start_at, stop_at, along):
    return lax.slice_in_dim(array, start_at, stop_at, axis=array.ndim + along)


def ppm_sweep(tracer_pad, depth_pad, flows, along):
    count = flows.shape[flows.ndim + along] - 1
    left_cell = cut_along(tracer_pad, 1, count + 4, along)
    right_cell = cut_along(tracer_pad, 2, count + 5, along)
    edge_vals = (7.0 / 12.0) * (left_cell + right_cell) - (1.0 / 12.0) * (cut_along(tracer_pad, 0, count + 3, along) + cut_along(tracer_pad, 3, count + 6, along))
    edge_vals = jnp.clip(edge_vals, jnp.minimum(left_cell, right_cell), jnp.maximum(left_cell, right_cell))
    centre = cut_along(tracer_pad, 2, count + 4, along)
    left_dev = cut_along(edge_vals, 0, count + 2, along) - centre
    right_dev = cut_along(edge_vals, 1, count + 3, along) - centre
    left_lim = jnp.clip(left_dev, -2.0 * jnp.abs(right_dev), 2.0 * jnp.abs(right_dev))
    right_lim = jnp.clip(right_dev, -2.0 * jnp.abs(left_dev), 2.0 * jnp.abs(left_dev))
    left_edge = centre + left_lim
    right_edge = centre + right_lim
    slope_all = right_edge - left_edge
    curv_six = 6.0 * centre - 3.0 * (left_edge + right_edge)
    positive = flows > 0
    depth_up = jnp.where(positive, cut_along(depth_pad, 0, count + 1, along), cut_along(depth_pad, 1, count + 2, along))
    courant = jnp.abs(flows) / jnp.maximum(depth_up, 0.25)
    from_left = cut_along(right_edge, 0, count + 1, along) - 0.5 * courant * (cut_along(slope_all, 0, count + 1, along) - (1.0 - 2.0 * courant / 3.0) * cut_along(curv_six, 0, count + 1, along))
    from_right = cut_along(left_edge, 1, count + 2, along) + 0.5 * courant * (cut_along(slope_all, 1, count + 2, along) + (1.0 - 2.0 * courant / 3.0) * cut_along(curv_six, 1, count + 2, along))
    flux_face = flows * jnp.where(positive, from_left, from_right)
    depth_old = cut_along(depth_pad, 1, count + 1, along)
    tracer_old = cut_along(tracer_pad, 3, count + 3, along)
    depth_new = depth_old + cut_along(flows, 0, count, along) - cut_along(flows, 1, count + 1, along)
    content = depth_old * tracer_old + cut_along(flux_face, 0, count, along) - cut_along(flux_face, 1, count + 1, along)
    return content / depth_new, depth_new


def zonal_and_vertical(field, depth, record, sea_mask):
    east_faces = record[0] * (sea_mask * jnp.roll(sea_mask, -1, axis=1))[None]
    flows = jnp.concatenate([east_faces[..., -1:], east_faces], axis=-1)
    tracer_pad = jnp.concatenate([field[..., -3:], field, field[..., :3]], axis=-1)
    depth_pad = jnp.concatenate([depth[..., -1:], depth, depth[..., :1]], axis=-1)
    field, depth = ppm_sweep(tracer_pad, depth_pad, flows, -1)
    tracer_pad = jnp.concatenate([field[:, :1]] * 3 + [field] + [field[:, -1:]] * 3, axis=1)
    depth_pad = jnp.concatenate([depth[:1], depth, depth[-1:]], axis=0)
    down_faces = record[2] * sea_mask[None]
    flows = jnp.concatenate([jnp.zeros_like(down_faces[:1]), down_faces], axis=0)
    field, depth = ppm_sweep(tracer_pad, depth_pad, flows, -3)
    return field


def reference(tracers, transports, thickness, owner, land_sea, pairs, rates):
    sea_mask = land_sea.astype(jnp.float32)
    records = [jnp.concatenate([transports[step, owner[step]], thickness[step, owner[step]][None]], axis=0) for step in range(STEPS)]
    groups = TRACERS // TRC_DEV
    local_pairs = (pairs.reshape(groups, TRC_DEV) - (jnp.arange(groups, dtype=jnp.int32) * TRC_DEV)[:, None]).astype(jnp.int32)
    sea_pad = jnp.pad(sea_mask, ((1, 1), (0, 0)))
    face_mask = sea_pad[:-1] * sea_pad[1:]

    def one_group(inputs):
        field, partner_idx, rate_group = inputs
        for record in records:
            tracer_pad = jnp.pad(field, ((0, 0), (0, 0), (3, 3), (0, 0)))
            depth_pad = jnp.pad(record[3], ((0, 0), (1, 1), (0, 0)))
            north_faces = jnp.concatenate([record[1], jnp.zeros_like(record[1][:, :1])], axis=1) * face_mask[None]
            field, depth = ppm_sweep(tracer_pad, depth_pad, north_faces, -2)
            field = zonal_and_vertical(field, depth, record, sea_mask)
            partner = field[partner_idx]
            field = field + sea_mask[None, None] * rate_group[:, None, None, None] * (partner - field)
        return field

    shaped = tracers.reshape(groups, TRC_DEV, LEV, NLAT, LON)
    result = lax.map(one_group, (shaped, local_pairs, rates.reshape(groups, TRC_DEV)))
    return result.reshape(TRACERS, LEV, NLAT, LON)
```

```python
import functools

import jax
import jax.numpy as jnp
from jax import lax
from jax.experimental import pallas as pl
from jax.experimental.pallas import tpu as pltpu
from jax.sharding import PartitionSpec as P

MESH = pl.DeviceIdType.MESH
TRC, LEV, ROWS, LON, STEPS, RING = 8, 4, 8, 512, 2, 16
BLK = 128
F32 = jnp.float32

GROUPS = (((0, 1), (0, -1)), ((0, 0), (0, 2)), ((1, 1), (1, -1)), ((1, 0), (1, 2)))


def limited(left, right):
    two_l, two_r = 2.0 * jnp.abs(left), 2.0 * jnp.abs(right)
    return (
        jnp.minimum(jnp.maximum(left, -two_r), two_r),
        jnp.minimum(jnp.maximum(right, -two_l), two_l),
    )


def edge_dev(before, here, after):
    dev = 0.5 * here + (1.0 / 12.0) * (before - after)
    return jnp.minimum(jnp.maximum(dev, jnp.minimum(here, 0.0)), jnp.maximum(here, 0.0))


def face_terms(flow, depth_up):
    courant = jnp.abs(flow) / jnp.maximum(depth_up, 0.25)
    rest = 1.0 - courant
    scaled = flow * rest
    return scaled * rest, -courant * scaled


def kernel(
    tracers, transports, thickness, owner, land_sea, pairs, rates, out,
    stage, halo_rec, recv0, recv1, recv2, recv3, recv_halo0, recv_halo1, sel_a, sel_b, rec_a, rec_b, sea_int, sea_halo_int,
    field_a, field_b, mid, mid2, done,
    c_mer, c_zon, c_ver, w_mer, w_zon, w_ver, depth,
    owner_s, pairs_s, rates_s,
    local_sem, send_sem, recv_sem,
):
    recv, recv_halo = (recv0, recv1, recv2, recv3), (recv_halo0, recv_halo1)
    lat, me = lax.axis_index("lat"), lax.axis_index("trc")
    my_y, my_z = me // 4, me % 4
    north, south = lax.rem(lat + 1, RING), lax.rem(lat + RING - 1, RING)

    def lanes(y):
        return pl.ds(pl.multiple_of(y * BLK, BLK), BLK)

    barrier = pltpu.get_barrier_semaphore()

    def greet(k, _):
        peer = lax.rem(me + k, RING)
        pl.semaphore_signal(barrier, inc=1, device_id={"trc": peer}, device_id_type=MESH)
        return 0

    for beside in (north, south):
        pl.semaphore_signal(barrier, inc=1, device_id={"lat": beside}, device_id_type=MESH)
    lax.fori_loop(1, RING, greet, 0)

    stages = []
    for g, fields in enumerate(GROUPS):
        copies = []
        for f, (s, k) in enumerate(fields):
            source = thickness.at[s, 0] if k < 0 else transports.at[s, 0, k]
            for y in range(4):
                copies.append(
                    pltpu.make_async_copy(
                        source.at[:, :, pl.ds(y * BLK, BLK)],
                        stage.at[g, pl.ds(4 * y, 4), f],
                        local_sem.at[8 * g + 4 * f + y],
                    )
                )
        for copy in copies:
            copy.start()
        stages.append(copies)
    smalls = [
        pltpu.make_async_copy(owner, owner_s, local_sem.at[32]),
        pltpu.make_async_copy(pairs, pairs_s, local_sem.at[33]),
        pltpu.make_async_copy(rates, rates_s, local_sem.at[34]),
        pltpu.make_async_copy(land_sea, sea_int, local_sem.at[35]),
    ]
    loads = [
        pltpu.make_async_copy(
            tracers.at[t], field_a.at[:, pl.ds(3, ROWS), t], local_sem.at[36 + t]
        )
        for t in range(TRC)
    ]
    for copy in smalls + loads:
        copy.start()

    pl.semaphore_wait(barrier, RING + 1)

    def to_peers(source, target, sem):
        def one(k, _):
            peer = lax.rem(me + k, RING)
            pltpu.make_async_remote_copy(
                source(peer), target, send_sem.at[sem], recv_sem.at[sem],
                device_id={"trc": peer}, device_id_type=MESH,
            ).start()
            return 0

        lax.fori_loop(1, RING, one, 0)

    def all_bytes(sems, like):
        pltpu.make_async_copy(like, like, sems).wait()

    like15, like30 = recv_halo0.at[pl.ds(0, 15)], recv0.at[pl.ds(0, 15)]
    like45 = stage.at[pl.ds(0, 3), pl.ds(0, 15), 0]

    def beside_copy(source, target, sem, where):
        return pltpu.make_async_remote_copy(
            source, target, send_sem.at[sem], recv_sem.at[sem],
            device_id={"lat": where}, device_id_type=MESH,
        )

    def scatter(g):
        for copy in stages[g]:
            copy.wait()
        to_peers(lambda peer: stage.at[g, peer], recv[g].at[me], g)
        recv[g][me] = stage[g, me]

    scatter(0)
    rows = [
        beside_copy(thickness.at[:, 0, :, pl.ds(7, 1)], halo_rec.at[:, :, pl.ds(0, 1)], 10, north),
        beside_copy(thickness.at[:, 0, :, pl.ds(0, 1)], halo_rec.at[:, :, pl.ds(1, 1)], 11, south),
        beside_copy(transports.at[:, 0, 1, :, pl.ds(0, 1)], halo_rec.at[:, :, pl.ds(2, 1)], 12, south),
        beside_copy(land_sea.at[pl.ds(7, 1)], sea_halo_int.at[pl.ds(0, 1)], 13, north),
        beside_copy(land_sea.at[pl.ds(0, 1)], sea_halo_int.at[pl.ds(1, 1)], 14, south),
    ]
    for copy in rows:
        copy.start()
    scatter(1)
    for copy in rows[:3]:
        copy.wait()
    for s in range(STEPS):
        to_peers(lambda peer: halo_rec.at[s, peer % 4, :, lanes(peer // 4)], recv_halo[s].at[me], 4 + s)
        recv_halo[s][me] = halo_rec[s, my_z, :, lanes(my_y)]
    scatter(2)
    scatter(3)

    def field_halos(field, sem):
        return [
            beside_copy(field.at[:, pl.ds(8, 3)], field.at[:, pl.ds(0, 3)], sem, north),
            beside_copy(field.at[:, pl.ds(3, 3)], field.at[:, pl.ds(11, 3)], sem + 1, south),
        ]

    def clear_ends(field):
        @pl.when(lat == 0)
        def _():
            field[:, 0:3] = jnp.zeros((LEV, 3, TRC, LON), F32)

        @pl.when(lat == RING - 1)
        def _():
            field[:, 11:14] = jnp.zeros((LEV, 3, TRC, LON), F32)

    for copy in loads:
        copy.wait()
    halos = field_halos(field_a, 15)
    for copy in halos:
        copy.start()
    for copy in smalls:
        copy.wait()

    def gather(g):
        s, first = g // 2, g % 2 == 0
        all_bytes(recv_sem.at[g], like30)
        if first:
            all_bytes(recv_sem.at[4 + s], like15)
        from_slot = owner_s[s]
        chosen = recv[g][from_slot]
        if first:
            beside = recv_halo[s][from_slot]
            sel_a[s, 0:2] = chosen
            sel_a[s, 2] = beside
            rec_a[s, 0:2, my_z, :, lanes(my_y)] = chosen
            rec_a[s, 2, my_z, :, lanes(my_y)] = beside
            to_peers(lambda peer: sel_a.at[s], rec_a.at[s, :, my_z, :, lanes(my_y)], 6 + g)
        else:
            sel_b[s] = chosen
            rec_b[s, :, my_z, :, lanes(my_y)] = chosen
            to_peers(lambda peer: sel_b.at[s], rec_b.at[s, :, my_z, :, lanes(my_y)], 6 + g)

    gather(0)
    gather(1)
    gather(2)
    gather(3)

    for copy in rows[3:]:
        copy.wait()
    sub = lax.broadcasted_iota(jnp.int32, (ROWS, LON), 0)
    sea = sea_int[...].astype(F32)
    sea_s = jnp.where(lat > 0, sea_halo_int[0:1].astype(F32), 0.0)
    sea_n = jnp.where(lat < RING - 1, sea_halo_int[1:2].astype(F32), 0.0)
    mask_mer = sea * jnp.where(sub == 0, sea_s, pltpu.roll(sea, 1, axis=0))
    mask_top = sea[7:8] * sea_n
    mask_zon = sea * pltpu.roll(sea, LON - 1, axis=1)
    sub1 = lax.broadcasted_iota(jnp.int32, (TRC, BLK), 0)
    partner = jnp.zeros((TRC, BLK), jnp.int32)
    rate = jnp.zeros((TRC, BLK), F32)
    for i in range(TRC):
        partner = jnp.where(sub1 == i, pairs_s[i] - me * TRC, partner)
        rate = jnp.where(sub1 == i, rates_s[i], rate)

    def mer_terms(s):
        def level(l, _):
            flow0, h, x = rec_a[s, 0, l], rec_a[s, 1, l], rec_a[s, 2, l]
            flow = flow0 * mask_mer
            below = jnp.where(sub == 0, x[0:1], pltpu.roll(h, 1, axis=0))
            near, far = face_terms(flow, jnp.where(flow > 0, below, h))
            c_mer[0, l, 0:8], c_mer[1, l, 0:8], c_mer[2, l, 0:8] = flow, near, far
            top = x[2:3] * mask_top
            near, far = face_terms(top, jnp.where(top > 0, h[7:8], x[1:2]))
            c_mer[0, l, 8:9], c_mer[1, l, 8:9], c_mer[2, l, 8:9] = top, near, far
            h_new = h + flow - jnp.where(sub == 7, top, pltpu.roll(flow, 7, axis=0))
            inv = 1.0 / h_new
            w_mer[0, l], w_mer[1, l] = h * inv, inv
            depth[l] = h_new
            return 0

        lax.fori_loop(0, LEV, level, 0)

    def zon_terms(s):
        def level(l, _):
            h = depth[l]
            east = rec_b[s, 0, l] * mask_zon
            flow = pltpu.roll(east, 1, axis=1)
            near, far = face_terms(flow, jnp.where(flow > 0, pltpu.roll(h, 1, axis=1), h))
            c_zon[0, l], c_zon[1, l], c_zon[2, l] = flow, near, far
            h_new = h + flow - east
            inv = 1.0 / h_new
            w_zon[0, l], w_zon[1, l] = h * inv, inv
            depth[l] = h_new
            return 0

        lax.fori_loop(0, LEV, level, 0)

    def ver_terms(s):
        flow_in = jnp.zeros((ROWS, LON), F32)
        for l in range(LEV):
            h = depth[l]
            flow = rec_b[s, 1, l] * sea
            c_ver[0, l] = flow
            if l < LEV - 1:
                c_ver[1, l], c_ver[2, l] = face_terms(flow, jnp.where(flow > 0, h, depth[l + 1]))
            inv = 1.0 / (h + flow_in - flow)
            w_ver[0, l], w_ver[1, l] = h * inv, inv
            flow_in = flow

    def wide(ref, *at):
        return jnp.broadcast_to(ref[at], (TRC, ref[at].shape[-1]))

    def flux(flow, near, far, q0, r0, l0, q1, l1, r1):
        up = flow > 0
        return (
            flow * jnp.where(up, q0, q1)
            + near * jnp.where(up, r0, l1)
            + far * jnp.where(up, l0, r1)
        )

    def meridional(field):
        def column(i, _):
            l, y = i // 4, lanes(i % 4)
            q = [field[l, j, :, y] for j in range(14)]
            d = [None] + [q[j] - q[j - 1] for j in range(1, 14)]
            e = {f: edge_dev(d[f - 1], d[f], d[f + 1]) for f in range(2, 13)}
            dev = {j: limited(e[j] - d[j], e[j + 1]) for j in range(2, 12)}
            across = []
            for f in range(3, 12):
                r = pl.ds(f - 3, 1)
                terms = [wide(c_mer, k, l, r, y) for k in range(3)]
                (l0, r0), (l1, r1) = dev[f - 1], dev[f]
                across.append(flux(*terms, q[f - 1], r0, l0, q[f], l1, r1))
            for r in range(ROWS):
                kept, inv = (wide(w_mer, k, l, pl.ds(r, 1), y) for k in range(2))
                mid[l, r, :, y] = kept * q[r + 3] + inv * (across[r] - across[r + 1])
            return 0

        lax.fori_loop(0, LEV * 4, column, 0)

    def zonal_row(r):
        def level(l, _):
            q = mid[l, r]
            before = pltpu.roll(q, 1, axis=1)
            d = q - before
            e = edge_dev(pltpu.roll(d, 1, axis=1), d, pltpu.roll(d, LON - 1, axis=1))
            left, right = limited(e - d, pltpu.roll(e, LON - 1, axis=1))
            at = pl.ds(r, 1)
            terms = [wide(c_zon, k, l, at) for k in range(3)]
            across = flux(*terms, before, pltpu.roll(right, 1, axis=1), pltpu.roll(left, 1, axis=1), q, left, right)
            kept, inv = (wide(w_zon, k, l, at) for k in range(2))
            mid2[l] = kept * q + inv * (across - pltpu.roll(across, LON - 1, axis=1))
            return 0

        lax.fori_loop(0, LEV, level, 0)

    def vertical_row(r, target, offset):
        def block(b, _):
            y, at = lanes(b), pl.ds(r, 1)
            q = [mid2[l, :, y] for l in range(LEV)]
            none = jnp.zeros((TRC, BLK), F32)
            d = [none] + [q[l] - q[l - 1] for l in range(1, LEV)] + [none]
            e = [none] + [edge_dev(d[f - 1], d[f], d[f + 1]) for f in range(1, LEV)] + [none]
            dev = [(none, none)] + [limited(e[l] - d[l], e[l + 1]) for l in range(1, LEV - 1)] + [(none, none)]
            across = [None]
            for f in range(1, LEV):
                terms = [wide(c_ver, k, f - 1, at, y) for k in range(3)]
                (l0, r0), (l1, r1) = dev[f - 1], dev[f]
                across.append(flux(*terms, q[f - 1], r0, l0, q[f], l1, r1))
            across.append(wide(c_ver, 0, LEV - 1, at, y) * q[LEV - 1])
            share = rate * jnp.broadcast_to(sea_f[at, y], (TRC, BLK))
            for l in range(LEV):
                kept, inv = (wide(w_ver, k, l, at, y) for k in range(2))
                gain = -across[l + 1] if l == 0 else across[l] - across[l + 1]
                new = kept * q[l] + inv * gain
                other = jnp.take_along_axis(new, partner, axis=0)
                target[l, offset + r, :, y] = new + share * (other - new)
            return 0

        lax.fori_loop(0, 4, block, 0)

    sea_f = depth.at[LEV]
    sea_f[...] = sea

    def run_rows(first, last, target, offset):
        for r in range(first, last):
            zonal_row(r)
            vertical_row(r, target, offset)

    all_bytes(recv_sem.at[6], like45)
    mer_terms(0)
    for copy in halos:
        copy.wait()
    clear_ends(field_a)
    meridional(field_a)
    all_bytes(recv_sem.at[7], like30)
    zon_terms(0)
    ver_terms(0)
    halos = field_halos(field_b, 17)
    run_rows(0, 3, field_b, 3)
    halos[1].start()
    run_rows(5, 8, field_b, 3)
    halos[0].start()
    run_rows(3, 5, field_b, 3)

    all_bytes(recv_sem.at[8], like45)
    mer_terms(1)
    for copy in halos:
        copy.wait()
    clear_ends(field_b)
    meridional(field_b)
    all_bytes(recv_sem.at[9], like30)
    zon_terms(1)
    ver_terms(1)
    run_rows(0, ROWS, done, 0)
    stores = [
        pltpu.make_async_copy(done.at[:, :, t], out.at[t], local_sem.at[36 + t])
        for t in range(TRC)
    ]
    for copy in stores:
        copy.start()
    for g, like in ((0, like30), (1, like30), (2, like30), (3, like30), (4, like15), (5, like15),
                    (6, like45), (7, like30), (8, like45), (9, like30)):
        all_bytes(send_sem.at[g], like)
    for copy in stores:
        copy.wait()


def per_device(*args):
    any_space = pl.BlockSpec(memory_space=pl.ANY)
    vmem = pltpu.VMEM
    return pl.pallas_call(
        kernel,
        out_shape=jax.ShapeDtypeStruct((TRC, LEV, ROWS, LON), F32),
        in_specs=[any_space] * 7,
        out_specs=any_space,
        scratch_shapes=[
            vmem((4, RING, 2, ROWS, BLK), F32),
            vmem((STEPS, LEV, ROWS, LON), F32),
            *[vmem((RING, 2, ROWS, BLK), F32)] * 4,
            *[vmem((RING, ROWS, BLK), F32)] * STEPS,
            vmem((STEPS, 3, ROWS, BLK), F32),
            vmem((STEPS, 2, ROWS, BLK), F32),
            vmem((STEPS, 3, LEV, ROWS, LON), F32),
            vmem((STEPS, 2, LEV, ROWS, LON), F32),
            vmem((ROWS, LON), jnp.int32),
            vmem((ROWS, LON), jnp.int32),
            vmem((LEV, 14, TRC, LON), F32),
            vmem((LEV, 14, TRC, LON), F32),
            vmem((LEV, ROWS, TRC, LON), F32),
            vmem((LEV, TRC, LON), F32),
            vmem((LEV, ROWS, TRC, LON), F32),
            vmem((3, LEV, 2 * ROWS, LON), F32),
            vmem((3, LEV, ROWS, LON), F32),
            vmem((3, LEV, ROWS, LON), F32),
            vmem((2, LEV, ROWS, LON), F32),
            vmem((2, LEV, ROWS, LON), F32),
            vmem((2, LEV, ROWS, LON), F32),
            vmem((LEV + 1, ROWS, LON), F32),
            pltpu.SMEM((STEPS,), jnp.int32),
            pltpu.SMEM((TRC,), jnp.int32),
            pltpu.SMEM((TRC,), F32),
            pltpu.SemaphoreType.DMA((44,)),
            pltpu.SemaphoreType.DMA((19,)),
            pltpu.SemaphoreType.DMA((19,)),
        ],
        compiler_params=pltpu.CompilerParams(
            collective_id=0, has_side_effects=True, vmem_limit_bytes=32 * 1024 * 1024
        ),
    )(*args)


def solution(mesh):
    placed = (
        P("trc", None, "lat", None),
        P(None, "trc", None, None, "lat", None),
        P(None, "trc", None, "lat", None),
        P(),
        P("lat", None),
        P("trc"),
        P("trc"),
    )
    return jax.shard_map(
        per_device,
        mesh=mesh,
        in_specs=placed,
        out_specs=P("trc", None, "lat", None),
        check_vma=False,
    )
```

```python
import functools

import jax
import jax.numpy as jnp
from jax import lax
from jax.experimental import pallas as pl
from jax.experimental.pallas import tpu as pltpu
from jax.sharding import PartitionSpec as P

MESH = pl.DeviceIdType.MESH
TRC, LEV, ROWS, LON, STEPS, RING = 8, 4, 8, 512, 2, 16
BLK = 128
F32 = jnp.float32

GROUPS = (((0, 1), (0, -1)), ((0, 0), (0, 2)), ((1, 1), (1, -1)), ((1, 0), (1, 2)))

TILES = (3, 2, 3, 2)


def limited(left, right):
    two_l, two_r = 2.0 * jnp.abs(left), 2.0 * jnp.abs(right)
    return (
        jnp.minimum(jnp.maximum(left, -two_r), two_r),
        jnp.minimum(jnp.maximum(right, -two_l), two_l),
    )


def edge_dev(before, here, after):
    dev = 0.5 * here + (1.0 / 12.0) * (before - after)
    return jnp.minimum(jnp.maximum(dev, jnp.minimum(here, 0.0)), jnp.maximum(here, 0.0))


def face_terms(flow, depth_up):
    courant = jnp.abs(flow) / jnp.maximum(depth_up, 0.25)
    rest = 1.0 - courant
    scaled = flow * rest
    return scaled * rest, -courant * scaled


def kernel(
    tracers, transports, thickness, owner, land_sea, pairs, rates, out,
    stage, halo_rec, recv0, recv_halo0, along_y1, along_y2, along_y3, along_z1, along_z2, along_z3,
    quarter1, quarter2, quarter3, part1, part2, part3, sel, rec_a, rec_b, sea_int, sea_halo_int,
    field_a, field_b, mid, mid2, done,
    c_mer, c_zon, c_ver, w_mer, w_zon, w_ver, depth,
    owner_s, pairs_s, rates_s,
    local_sem, send_sem, recv_sem,
):
    along_y, along_z = (None, along_y1, along_y2, along_y3), (None, along_z1, along_z2, along_z3)
    quarter, part = (None, quarter1, quarter2, quarter3), (None, part1, part2, part3)
    lat, me = lax.axis_index("lat"), lax.axis_index("trc")
    my_y, my_z = me // 4, me % 4
    north, south = lax.rem(lat + 1, RING), lax.rem(lat + RING - 1, RING)

    def lanes(y):
        return pl.ds(pl.multiple_of(y * BLK, BLK), BLK)

    barrier = pltpu.get_barrier_semaphore()

    def greet(k, _):
        peer = lax.rem(me + k, RING)
        pl.semaphore_signal(barrier, inc=1, device_id={"trc": peer}, device_id_type=MESH)
        return 0

    for beside in (north, south):
        pl.semaphore_signal(barrier, inc=1, device_id={"lat": beside}, device_id_type=MESH)
    lax.fori_loop(1, RING, greet, 0)

    stages = []
    for g, fields in enumerate(GROUPS):
        copies = []
        for f, (s, k) in enumerate(fields):
            source = thickness.at[s, 0] if k < 0 else transports.at[s, 0, k]
            for y in range(4):
                copies.append(
                    pltpu.make_async_copy(
                        source.at[:, :, pl.ds(y * BLK, BLK)],
                        stage.at[g, pl.ds(4 * y, 4), f],
                        local_sem.at[8 * g + 4 * f + y],
                    )
                )
        for copy in copies:
            copy.start()
        stages.append(copies)
    smalls = [
        pltpu.make_async_copy(owner, owner_s, local_sem.at[32]),
        pltpu.make_async_copy(pairs, pairs_s, local_sem.at[33]),
        pltpu.make_async_copy(rates, rates_s, local_sem.at[34]),
        pltpu.make_async_copy(land_sea, sea_int, local_sem.at[35]),
    ]
    loads = [
        pltpu.make_async_copy(
            tracers.at[t], field_a.at[:, pl.ds(3, ROWS), t], local_sem.at[36 + t]
        )
        for t in range(TRC)
    ]
    for copy in smalls + loads:
        copy.start()

    pl.semaphore_wait(barrier, RING + 1)

    def one_copy(source, target, sem, **where):
        return pltpu.make_async_remote_copy(
            source, target, send_sem.at[sem], recv_sem.at[sem], device_id=where, device_id_type=MESH
        )

    def to_peers(source, target, sem):
        def one(k, _):
            peer = lax.rem(me + k, RING)
            one_copy(source(peer), target, sem, trc=peer).start()
            return 0

        lax.fori_loop(1, RING, one, 0)

    def along(axis, source, target, sem):
        for k in (2, 1, 3):
            if axis == "y":
                at = lax.rem(my_y + k, 4)
                one_copy(source(at), target, sem, trc=at * 4 + my_z).start()
            else:
                at = lax.rem(my_z + k, 4)
                one_copy(source(at), target, sem, trc=my_y * 4 + at).start()

    def all_bytes(sems, like):
        pltpu.make_async_copy(like, like, sems).wait()

    three = pl.ds(0, 3)
    likes = {0: recv0.at[pl.ds(0, 15)], 1: recv_halo0.at[pl.ds(0, 15)], 2: stage.at[three, pl.ds(0, 15), 0]}
    for g in (1, 2, 3):
        first = 8 + 4 * g
        likes[first] = likes[first + 3] = along_y[g].at[three]
        likes[first + 1] = likes[first + 2] = along_z[g].at[three]

    def arrived(sem):
        all_bytes(recv_sem.at[sem], likes[sem])

    def staged(g):
        for copy in stages[g]:
            copy.wait()

    def scatter_y(g):
        staged(g)
        own = pl.ds(4 * my_y, 4)
        if TILES[g] == 3:
            along("y", lambda y: stage.at[g, pl.ds(4 * y, 4)], along_y[g].at[my_y, :, pl.ds(0, 2)], 8 + 4 * g)
            along("y", lambda y: halo_rec.at[1, :, :, lanes(y)], along_y[g].at[my_y, :, 2], 8 + 4 * g)
            along_y[g][my_y, :, 0:2] = stage[g, own]
            along_y[g][my_y, :, 2] = halo_rec[1, :, :, lanes(my_y)]
        else:
            along("y", lambda y: stage.at[g, pl.ds(4 * y, 4)], along_y[g].at[my_y], 8 + 4 * g)
            along_y[g][my_y] = stage[g, own]

    def scatter_z(g):
        arrived(8 + 4 * g)
        quarter[g][...] = along_y[g][owner_s[g // 2] // 4]
        along("z", lambda z: quarter[g].at[z], along_z[g].at[my_z], 9 + 4 * g)
        along_z[g][my_z] = quarter[g][my_z]

    def gather_z(g):
        arrived(9 + 4 * g)
        part[g][my_z] = along_z[g][lax.rem(owner_s[g // 2], 4)]
        along("z", lambda z: part[g].at[my_z], part[g].at[my_z], 10 + 4 * g)

    def gather_y(g):
        arrived(10 + 4 * g)
        rec = (rec_a if TILES[g] == 3 else rec_b).at[g // 2]
        along("y", lambda y: part[g], rec.at[:, :, :, lanes(my_y)], 11 + 4 * g)
        rec[:, :, :, lanes(my_y)] = part[g][...]

    staged(0)
    to_peers(lambda peer: stage.at[0, peer], recv0.at[me], 0)
    recv0[me] = stage[0, me]
    one, top = pl.ds(0, 1), pl.ds(7, 1)
    rows = [
        one_copy(thickness.at[:, 0, :, top], halo_rec.at[:, :, pl.ds(0, 1)], 3, lat=north),
        one_copy(thickness.at[:, 0, :, one], halo_rec.at[:, :, pl.ds(1, 1)], 4, lat=south),
        one_copy(transports.at[:, 0, 1, :, one], halo_rec.at[:, :, pl.ds(2, 1)], 5, lat=south),
        one_copy(land_sea.at[top], sea_halo_int.at[pl.ds(0, 1)], 6, lat=north),
        one_copy(land_sea.at[one], sea_halo_int.at[pl.ds(1, 1)], 7, lat=south),
    ]
    for copy in rows:
        copy.start()
    scatter_y(1)
    for copy in smalls:
        copy.wait()
    for copy in rows[:3]:
        copy.wait()
    to_peers(lambda peer: halo_rec.at[0, peer % 4, :, lanes(peer // 4)], recv_halo0.at[me], 1)
    recv_halo0[me] = halo_rec[0, my_z, :, lanes(my_y)]
    scatter_y(2)
    scatter_y(3)
    scatter_z(1)

    def field_halos(field, sem):
        return [
            one_copy(field.at[:, pl.ds(8, 3)], field.at[:, pl.ds(0, 3)], sem, lat=north),
            one_copy(field.at[:, pl.ds(3, 3)], field.at[:, pl.ds(11, 3)], sem + 1, lat=south),
        ]

    def clear_ends(field):
        @pl.when(lat == 0)
        def _():
            field[:, 0:3] = jnp.zeros((LEV, 3, TRC, LON), F32)

        @pl.when(lat == RING - 1)
        def _():
            field[:, 11:14] = jnp.zeros((LEV, 3, TRC, LON), F32)

    for copy in loads:
        copy.wait()
    halos = field_halos(field_a, 8)
    for copy in halos:
        copy.start()

    arrived(0)
    arrived(1)
    sel[0:2] = recv0[owner_s[0]]
    sel[2] = recv_halo0[owner_s[0]]
    to_peers(lambda peer: sel, rec_a.at[0, my_z, :, :, lanes(my_y)], 2)
    rec_a[0, my_z, :, :, lanes(my_y)] = sel[...]
    scatter_z(2)
    scatter_z(3)
    gather_z(1)
    gather_z(2)
    gather_z(3)
    gather_y(1)

    for copy in rows[3:]:
        copy.wait_recv()
    sub = lax.broadcasted_iota(jnp.int32, (ROWS, LON), 0)
    sea = sea_int[...].astype(F32)
    sea_s = jnp.where(lat > 0, sea_halo_int[0:1].astype(F32), 0.0)
    sea_n = jnp.where(lat < RING - 1, sea_halo_int[1:2].astype(F32), 0.0)
    mask_mer = sea * jnp.where(sub == 0, sea_s, pltpu.roll(sea, 1, axis=0))
    mask_top = sea[7:8] * sea_n
    mask_zon = sea * pltpu.roll(sea, LON - 1, axis=1)
    sub1 = lax.broadcasted_iota(jnp.int32, (TRC, BLK), 0)
    partner = jnp.zeros((TRC, BLK), jnp.int32)
    rate = jnp.zeros((TRC, BLK), F32)
    for i in range(TRC):
        partner = jnp.where(sub1 == i, pairs_s[i] - me * TRC, partner)
        rate = jnp.where(sub1 == i, rates_s[i], rate)

    def mer_terms(s):
        def level(l, _):
            flow0, h, x = rec_a[s, l, 0], rec_a[s, l, 1], rec_a[s, l, 2]
            flow = flow0 * mask_mer
            below = jnp.where(sub == 0, x[0:1], pltpu.roll(h, 1, axis=0))
            near, far = face_terms(flow, jnp.where(flow > 0, below, h))
            c_mer[0, l, 0:8], c_mer[1, l, 0:8], c_mer[2, l, 0:8] = flow, near, far
            top = x[2:3] * mask_top
            near, far = face_terms(top, jnp.where(top > 0, h[7:8], x[1:2]))
            c_mer[0, l, 8:9], c_mer[1, l, 8:9], c_mer[2, l, 8:9] = top, near, far
            h_new = h + flow - jnp.where(sub == 7, top, pltpu.roll(flow, 7, axis=0))
            inv = 1.0 / h_new
            w_mer[0, l], w_mer[1, l] = h * inv, inv
            depth[l] = h_new
            return 0

        lax.fori_loop(0, LEV, level, 0)

    def zon_terms(s):
        def level(l, _):
            h = depth[l]
            east = rec_b[s, l, 0] * mask_zon
            west = pltpu.roll(east, 1, axis=1)
            h_new = h + west - east
            inv = 1.0 / h_new
            flow = jnp.maximum(east, 0.0)
            c_zon[0, l] = flow
            c_zon[1, l], c_zon[2, l] = face_terms(flow, h)
            flow = jnp.minimum(west, 0.0)
            c_zon[3, l] = flow
            c_zon[4, l], c_zon[5, l] = face_terms(flow, h)
            w_zon[0, l], w_zon[1, l] = h * inv, inv
            depth[l] = h_new
            return 0

        lax.fori_loop(0, LEV, level, 0)

    def ver_terms(s):
        flow_in = jnp.zeros((ROWS, LON), F32)
        for l in range(LEV):
            h = depth[l]
            flow = rec_b[s, l, 1] * sea
            c_ver[0, l] = flow
            if l < LEV - 1:
                c_ver[1, l], c_ver[2, l] = face_terms(flow, jnp.where(flow > 0, h, depth[l + 1]))
            inv = 1.0 / (h + flow_in - flow)
            w_ver[0, l], w_ver[1, l] = h * inv, inv
            flow_in = flow

    def wide(ref, *at):
        return jnp.broadcast_to(ref[at], (TRC, ref[at].shape[-1]))

    def flux(flow, near, far, q0, r0, l0, q1, l1, r1):
        up = flow > 0
        return (
            flow * jnp.where(up, q0, q1)
            + near * jnp.where(up, r0, l1)
            + far * jnp.where(up, l0, r1)
        )

    def meridional(field):
        def column(i, _):
            l, y = i // 4, lanes(i % 4)
            q = [field[l, j, :, y] for j in range(14)]
            d = [None] + [q[j] - q[j - 1] for j in range(1, 14)]
            e = {f: edge_dev(d[f - 1], d[f], d[f + 1]) for f in range(2, 13)}
            dev = {j: limited(e[j] - d[j], e[j + 1]) for j in range(2, 12)}
            across = []
            for f in range(3, 12):
                r = pl.ds(f - 3, 1)
                terms = [wide(c_mer, k, l, r, y) for k in range(3)]
                (l0, r0), (l1, r1) = dev[f - 1], dev[f]
                across.append(flux(*terms, q[f - 1], r0, l0, q[f], l1, r1))
            for r in range(ROWS):
                kept, inv = (wide(w_mer, k, l, pl.ds(r, 1), y) for k in range(2))
                mid[l, r, :, y] = kept * q[r + 3] + inv * (across[r] - across[r + 1])
            return 0

        lax.fori_loop(0, LEV * 4, column, 0)

    lane = lax.broadcasted_iota(jnp.int32, (TRC, BLK), 1)

    def shifted(tiles, by):
        turned = [pltpu.roll(tile, -by % BLK, axis=1) for tile in tiles]
        inside = lane < BLK - by if by > 0 else lane >= -by
        step = 1 if by > 0 else -1
        return [jnp.where(inside, turned[b], turned[(b + step) % 4]) for b in range(4)]

    def zonal_row(r):
        at = pl.ds(r, 1)
        for l in range(LEV):
            q = [mid[l, r, :, b * BLK : (b + 1) * BLK] for b in range(4)]
            west2, west, east, east2 = (shifted(q, by) for by in (-2, -1, 1, 2))
            out_east, out_west = [], []
            for b in range(4):
                d_w, d, d_e, d_ee = west[b] - west2[b], q[b] - west[b], east[b] - q[b], east2[b] - east[b]
                left, right = limited(edge_dev(d_w, d, d_e) - d, edge_dev(d, d_e, d_ee))
                v0, n0, f0, v1, n1, f1 = (wide(c_zon, k, l, at, pl.ds(b * BLK, BLK)) for k in range(6))
                out_east.append(v0 * q[b] + n0 * right + f0 * left)
                out_west.append(v1 * q[b] + n1 * left + f1 * right)
            from_west, from_east = shifted(out_east, -1), shifted(out_west, 1)
            for b in range(4):
                y = pl.ds(b * BLK, BLK)
                kept, inv = (wide(w_zon, k, l, at, y) for k in range(2))
                gain = (from_west[b] - out_east[b]) + (out_west[b] - from_east[b])
                mid2[l, :, y] = kept * q[b] + inv * gain

    def vertical_row(r, target, offset):
        def block(b, _):
            y, at = lanes(b), pl.ds(r, 1)
            q = [mid2[l, :, y] for l in range(LEV)]
            none = jnp.zeros((TRC, BLK), F32)
            d = [none] + [q[l] - q[l - 1] for l in range(1, LEV)] + [none]
            e = [none] + [edge_dev(d[f - 1], d[f], d[f + 1]) for f in range(1, LEV)] + [none]
            dev = [(none, none)] + [limited(e[l] - d[l], e[l + 1]) for l in range(1, LEV - 1)] + [(none, none)]
            across = [None]
            for f in range(1, LEV):
                terms = [wide(c_ver, k, f - 1, at, y) for k in range(3)]
                (l0, r0), (l1, r1) = dev[f - 1], dev[f]
                across.append(flux(*terms, q[f - 1], r0, l0, q[f], l1, r1))
            across.append(wide(c_ver, 0, LEV - 1, at, y) * q[LEV - 1])
            share = rate * jnp.broadcast_to(sea_f[at, y], (TRC, BLK))
            for l in range(LEV):
                kept, inv = (wide(w_ver, k, l, at, y) for k in range(2))
                gain = -across[l + 1] if l == 0 else across[l] - across[l + 1]
                new = kept * q[l] + inv * gain
                other = jnp.take_along_axis(new, partner, axis=0)
                target[l, offset + r, :, y] = new + share * (other - new)
            return 0

        lax.fori_loop(0, 4, block, 0)

    sea_f = depth.at[LEV]
    sea_f[...] = sea

    def run_rows(first, last, target, offset):
        for r in range(first, last):
            zonal_row(r)
            vertical_row(r, target, offset)

    arrived(2)
    mer_terms(0)
    for copy in halos:
        copy.wait()
    clear_ends(field_a)
    meridional(field_a)
    gather_y(2)
    gather_y(3)
    arrived(15)
    zon_terms(0)
    ver_terms(0)
    halos = field_halos(field_b, 10)
    run_rows(0, 3, field_b, 3)
    halos[1].start()
    run_rows(5, 8, field_b, 3)
    halos[0].start()
    run_rows(3, 5, field_b, 3)

    arrived(19)
    mer_terms(1)
    for copy in halos:
        copy.wait()
    clear_ends(field_b)
    meridional(field_b)
    arrived(23)
    zon_terms(1)
    ver_terms(1)
    run_rows(0, ROWS, done, 0)
    stores = [
        pltpu.make_async_copy(done.at[:, :, t], out.at[t], local_sem.at[36 + t])
        for t in range(TRC)
    ]
    for copy in stores:
        copy.start()
    for sem, like in likes.items():
        all_bytes(send_sem.at[sem], like)
    for copy in rows[3:]:
        copy.wait_send()
    for copy in stores:
        copy.wait()


def per_device(*args):
    any_space = pl.BlockSpec(memory_space=pl.ANY)
    vmem = pltpu.VMEM
    return pl.pallas_call(
        kernel,
        out_shape=jax.ShapeDtypeStruct((TRC, LEV, ROWS, LON), F32),
        in_specs=[any_space] * 7,
        out_specs=any_space,
        scratch_shapes=[
            vmem((4, RING, 2, ROWS, BLK), F32),
            vmem((STEPS, LEV, ROWS, LON), F32),
            vmem((RING, 2, ROWS, BLK), F32),
            vmem((RING, ROWS, BLK), F32),
            *[vmem((4, 4, n, ROWS, BLK), F32) for n in TILES[1:]],
            *[vmem((4, n, ROWS, BLK), F32) for n in TILES[1:]],
            *[vmem((4, n, ROWS, BLK), F32) for n in TILES[1:]],
            *[vmem((4, n, ROWS, BLK), F32) for n in TILES[1:]],
            vmem((3, ROWS, BLK), F32),
            vmem((STEPS, LEV, 3, ROWS, LON), F32),
            vmem((STEPS, LEV, 2, ROWS, LON), F32),
            vmem((ROWS, LON), jnp.int32),
            vmem((ROWS, LON), jnp.int32),
            vmem((LEV, 14, TRC, LON), F32),
            vmem((LEV, 14, TRC, LON), F32),
            vmem((LEV, ROWS, TRC, LON), F32),
            vmem((LEV, TRC, LON), F32),
            vmem((LEV, ROWS, TRC, LON), F32),
            vmem((3, LEV, 2 * ROWS, LON), F32),
            vmem((6, LEV, ROWS, LON), F32),
            vmem((3, LEV, ROWS, LON), F32),
            vmem((2, LEV, ROWS, LON), F32),
            vmem((2, LEV, ROWS, LON), F32),
            vmem((2, LEV, ROWS, LON), F32),
            vmem((LEV + 1, ROWS, LON), F32),
            pltpu.SMEM((STEPS,), jnp.int32),
            pltpu.SMEM((TRC,), jnp.int32),
            pltpu.SMEM((TRC,), F32),
            pltpu.SemaphoreType.DMA((44,)),
            pltpu.SemaphoreType.DMA((24,)),
            pltpu.SemaphoreType.DMA((24,)),
        ],
        compiler_params=pltpu.CompilerParams(
            collective_id=0, has_side_effects=True, vmem_limit_bytes=60 * 1024 * 1024
        ),
    )(*args)


def solution(mesh):
    placed = (
        P("trc", None, "lat", None),
        P(None, "trc", None, None, "lat", None),
        P(None, "trc", None, "lat", None),
        P(),
        P("lat", None),
        P("trc"),
        P("trc"),
    )
    return jax.shard_map(
        per_device,
        mesh=mesh,
        in_specs=placed,
        out_specs=P("trc", None, "lat", None),
        check_vma=False,
    )
```

```python
import functools

import jax
import jax.numpy as jnp
from jax import lax
from jax.experimental import pallas as pl
from jax.experimental.pallas import tpu as pltpu
from jax.sharding import PartitionSpec as P

MESH = pl.DeviceIdType.MESH
TRC, LEV, ROWS, LON, STEPS, RING = 8, 4, 8, 512, 2, 16
BLK = 128
F32 = jnp.float32

GROUPS = (((0, 1), (0, -1)), ((0, 0), (0, 2)), ((1, 1), (1, -1)), ((1, 0), (1, 2)))


def limited(left, right):
    two_l, two_r = 2.0 * jnp.abs(left), 2.0 * jnp.abs(right)
    return (
        jnp.minimum(jnp.maximum(left, -two_r), two_r),
        jnp.minimum(jnp.maximum(right, -two_l), two_l),
    )


def edge_dev(before, here, after):
    dev = 0.5 * here + (1.0 / 12.0) * (before - after)
    return jnp.minimum(jnp.maximum(dev, jnp.minimum(here, 0.0)), jnp.maximum(here, 0.0))


def face_terms(flow, depth_up):
    courant = jnp.abs(flow) / jnp.maximum(depth_up, 0.25)
    rest = 1.0 - courant
    scaled = flow * rest
    return scaled * rest, -courant * scaled


def kernel(
    tracers, transports, thickness, owner, land_sea, pairs, rates, out,
    stage, recv0, along_y1, along_y2, along_y3, along_z1, along_z2, along_z3,
    quarter1, quarter2, quarter3, part2, part3, part1, sel, border0, border1, rec_a, rec_b, sea_int, sea_halo_int,
    field_a, field_b, mid, mid2, done,
    c_mer, c_zon, c_ver, w_mer, w_zon, w_ver, depth,
    owner_s, pairs_s, rates_s,
    local_sem, send_sem, recv_sem,
):
    along_y, along_z = (None, along_y1, along_y2, along_y3), (None, along_z1, along_z2, along_z3)
    quarter, part = (None, quarter1, quarter2, quarter3), (None, part1, part2, part3)
    lat, me = lax.axis_index("lat"), lax.axis_index("trc")
    my_y, my_z = me // 4, me % 4
    north, south = lax.rem(lat + 1, RING), lax.rem(lat + RING - 1, RING)

    def lanes(y):
        return pl.ds(pl.multiple_of(y * BLK, BLK), BLK)

    barrier = pltpu.get_barrier_semaphore()

    def greet(k, _):
        peer = lax.rem(me + k, RING)
        pl.semaphore_signal(barrier, inc=1, device_id={"trc": peer}, device_id_type=MESH)
        return 0

    for beside in (north, south):
        pl.semaphore_signal(barrier, inc=1, device_id={"lat": beside}, device_id_type=MESH)
    lax.fori_loop(1, RING, greet, 0)

    stages = []
    for g, fields in enumerate(GROUPS):
        copies = []
        for f, (s, k) in enumerate(fields):
            source = thickness.at[s, 0] if k < 0 else transports.at[s, 0, k]
            for y in range(4):
                copies.append(
                    pltpu.make_async_copy(
                        source.at[:, :, pl.ds(y * BLK, BLK)],
                        stage.at[g, pl.ds(4 * y, 4), f],
                        local_sem.at[8 * g + 4 * f + y],
                    )
                )
        for copy in copies:
            copy.start()
        stages.append(copies)
    smalls = [
        pltpu.make_async_copy(owner, owner_s, local_sem.at[32]),
        pltpu.make_async_copy(pairs, pairs_s, local_sem.at[33]),
        pltpu.make_async_copy(rates, rates_s, local_sem.at[34]),
        pltpu.make_async_copy(land_sea, sea_int, local_sem.at[35]),
    ]
    loads = [
        pltpu.make_async_copy(
            tracers.at[t], field_a.at[:, pl.ds(3, ROWS), t], local_sem.at[36 + t]
        )
        for t in range(TRC)
    ]
    for copy in smalls + loads:
        copy.start()

    pl.semaphore_wait(barrier, RING + 1)

    def one_copy(source, target, sem, **where):
        return pltpu.make_async_remote_copy(
            source, target, send_sem.at[sem], recv_sem.at[sem], device_id=where, device_id_type=MESH
        )

    def to_peers(source, target, sem):
        def one(k, _):
            peer = lax.rem(me + k, RING)
            one_copy(source(peer), target, sem, trc=peer).start()
            return 0

        lax.fori_loop(1, RING, one, 0)

    def along(axis, source, target, sem):
        for k in (2, 1, 3):
            if axis == "y":
                at = lax.rem(my_y + k, 4)
                one_copy(source(at), target, sem, trc=at * 4 + my_z).start()
            else:
                at = lax.rem(my_z + k, 4)
                one_copy(source(at), target, sem, trc=my_y * 4 + at).start()

    def all_bytes(sems, like):
        pltpu.make_async_copy(like, like, sems).wait()

    for_north, for_south = pl.ds(0, 1), pl.ds(1, 2)

    def put_border(border, tile):
        border[0:1], border[1:2], border[2:3] = tile[1, 7:8], tile[1, 0:1], tile[0, 0:1]

    three = pl.ds(0, 3)
    likes = {
        0: recv0.at[pl.ds(0, 15)],
        1: recv0.at[pl.ds(0, 15)],
        2: rec_a.at[0, :, 2, for_north],
        3: rec_a.at[0, :, 2, for_south],
        4: part2.at[:, 2, for_north],
        5: part2.at[:, 2, for_south],
        12: along_y1.at[three],
        13: along_z1.at[three],
        15: along_y1.at[three],
        16: along_y2.at[three],
        17: along_z2.at[three],
        18: along_z2.at[three],
        19: rec_a.at[1, three],
        20: along_y3.at[three],
        21: along_z3.at[three],
        22: along_z3.at[three],
        23: along_y3.at[three],
    }

    def arrived(sem):
        all_bytes(recv_sem.at[sem], likes[sem])

    def staged(g):
        for copy in stages[g]:
            copy.wait()

    def scatter_y(g):
        staged(g)
        along("y", lambda y: stage.at[g, pl.ds(4 * y, 4)], along_y[g].at[my_y], 8 + 4 * g)
        along_y[g][my_y] = stage[g, pl.ds(4 * my_y, 4)]

    def scatter_z(g):
        arrived(8 + 4 * g)
        quarter[g][...] = along_y[g][owner_s[g // 2] // 4]
        if g == 1:
            along("z", lambda z: quarter1, along_z1.at[my_z], 13)
            along_z1[my_z] = quarter1[...]
        else:
            along("z", lambda z: quarter[g].at[z], along_z[g].at[my_z], 9 + 4 * g)
            along_z[g][my_z] = quarter[g][my_z]

    def gather_z(g):
        arrived(9 + 4 * g)
        chosen = along_z[g][lax.rem(owner_s[g // 2], 4)]
        if g == 1:
            part1[...] = chosen
            return
        both = pl.ds(0, 2)
        part[g][my_z, 0:2] = chosen
        along("z", lambda z: part[g].at[my_z, both], part[g].at[my_z, both], 10 + 4 * g)
        if g == 2:
            put_border(border1, chosen)
            for k in range(4):
                there = my_y * 4 + lax.rem(my_z + k, 4)
                one_copy(border1.at[for_north], part2.at[my_z, 2, for_north], 4, lat=north, trc=there).start()
                one_copy(border1.at[for_south], part2.at[my_z, 2, for_south], 5, lat=south, trc=there).start()

    def gather_y(g):
        if g > 1:
            arrived(10 + 4 * g)
        if g == 2:
            arrived(4)
            arrived(5)
        rec = (rec_a if g == 2 else rec_b).at[g // 2]
        along("y", lambda y: part[g], rec.at[:, :, :, lanes(my_y)], 11 + 4 * g)
        rec[:, :, :, lanes(my_y)] = part[g][...]

    staged(0)
    to_peers(lambda peer: stage.at[0, peer], recv0.at[me], 0)
    recv0[me] = stage[0, me]
    scatter_y(1)
    scatter_y(2)
    scatter_y(3)
    rows = [
        one_copy(land_sea.at[pl.ds(7, 1)], sea_halo_int.at[pl.ds(0, 1)], 6, lat=north),
        one_copy(land_sea.at[pl.ds(0, 1)], sea_halo_int.at[pl.ds(1, 1)], 7, lat=south),
    ]
    for copy in rows:
        copy.start()
    for copy in smalls:
        copy.wait()

    def field_halos(field, sem):
        return [
            one_copy(field.at[:, pl.ds(8, 3)], field.at[:, pl.ds(0, 3)], sem, lat=north),
            one_copy(field.at[:, pl.ds(3, 3)], field.at[:, pl.ds(11, 3)], sem + 1, lat=south),
        ]

    def clear_ends(field):
        @pl.when(lat == 0)
        def _():
            field[:, 0:3] = jnp.zeros((LEV, 3, TRC, LON), F32)

        @pl.when(lat == RING - 1)
        def _():
            field[:, 11:14] = jnp.zeros((LEV, 3, TRC, LON), F32)

    for copy in loads:
        copy.wait()
    halos = field_halos(field_a, 8)
    for copy in halos:
        copy.start()

    scatter_z(1)
    scatter_z(2)
    scatter_z(3)
    arrived(0)
    chosen = recv0[owner_s[0]]
    sel[...] = chosen
    put_border(border0, chosen)
    both = pl.ds(0, 2)
    to_peers(lambda peer: sel, rec_a.at[0, my_z, both, :, lanes(my_y)], 1)

    def borders(k, _):
        there = lax.rem(me + k, RING)
        for part_of, sem, where in ((for_north, 2, north), (for_south, 3, south)):
            target = rec_a.at[0, my_z, 2, part_of, lanes(my_y)]
            one_copy(border0.at[part_of], target, sem, lat=where, trc=there).start()
        return 0

    lax.fori_loop(0, RING, borders, 0)
    rec_a[0, my_z, 0:2, :, lanes(my_y)] = chosen
    gather_z(2)
    gather_z(3)
    gather_z(1)
    gather_y(1)

    for copy in rows:
        copy.wait_recv()
    sub = lax.broadcasted_iota(jnp.int32, (ROWS, LON), 0)
    sea = sea_int[...].astype(F32)
    sea_s = jnp.where(lat > 0, sea_halo_int[0:1].astype(F32), 0.0)
    sea_n = jnp.where(lat < RING - 1, sea_halo_int[1:2].astype(F32), 0.0)
    mask_mer = sea * jnp.where(sub == 0, sea_s, pltpu.roll(sea, 1, axis=0))
    mask_top = sea[7:8] * sea_n
    mask_zon = sea * pltpu.roll(sea, LON - 1, axis=1)
    sub1 = lax.broadcasted_iota(jnp.int32, (TRC, BLK), 0)
    partner = jnp.zeros((TRC, BLK), jnp.int32)
    rate = jnp.zeros((TRC, BLK), F32)
    for i in range(TRC):
        partner = jnp.where(sub1 == i, pairs_s[i] - me * TRC, partner)
        rate = jnp.where(sub1 == i, rates_s[i], rate)

    def mer_terms(s):
        def level(l, _):
            flow0, h, x = rec_a[s, l, 0], rec_a[s, l, 1], rec_a[s, l, 2]
            flow = flow0 * mask_mer
            below = jnp.where(sub == 0, x[0:1], pltpu.roll(h, 1, axis=0))
            near, far = face_terms(flow, jnp.where(flow > 0, below, h))
            c_mer[0, l, 0:8], c_mer[1, l, 0:8], c_mer[2, l, 0:8] = flow, near, far
            top = x[2:3] * mask_top
            near, far = face_terms(top, jnp.where(top > 0, h[7:8], x[1:2]))
            c_mer[0, l, 8:9], c_mer[1, l, 8:9], c_mer[2, l, 8:9] = top, near, far
            h_new = h + flow - jnp.where(sub == 7, top, pltpu.roll(flow, 7, axis=0))
            inv = 1.0 / h_new
            w_mer[0, l], w_mer[1, l] = h * inv, inv
            depth[l] = h_new
            return 0

        lax.fori_loop(0, LEV, level, 0)

    def zon_terms(s):
        def level(l, _):
            h = depth[l]
            east = rec_b[s, l, 0] * mask_zon
            west = pltpu.roll(east, 1, axis=1)
            h_new = h + west - east
            inv = 1.0 / h_new
            flow = jnp.maximum(east, 0.0)
            c_zon[0, l] = flow
            c_zon[1, l], c_zon[2, l] = face_terms(flow, h)
            flow = jnp.minimum(west, 0.0)
            c_zon[3, l] = flow
            c_zon[4, l], c_zon[5, l] = face_terms(flow, h)
            w_zon[0, l], w_zon[1, l] = h * inv, inv
            depth[l] = h_new
            return 0

        lax.fori_loop(0, LEV, level, 0)

    def ver_terms(s):
        flow_in = jnp.zeros((ROWS, LON), F32)
        for l in range(LEV):
            h = depth[l]
            flow = rec_b[s, l, 1] * sea
            c_ver[0, l] = flow
            if l < LEV - 1:
                c_ver[1, l], c_ver[2, l] = face_terms(flow, jnp.where(flow > 0, h, depth[l + 1]))
            inv = 1.0 / (h + flow_in - flow)
            w_ver[0, l], w_ver[1, l] = h * inv, inv
            flow_in = flow

    def wide(ref, *at):
        return jnp.broadcast_to(ref[at], (TRC, ref[at].shape[-1]))

    def flux(flow, near, far, q0, r0, l0, q1, l1, r1):
        up = flow > 0
        return (
            flow * jnp.where(up, q0, q1)
            + near * jnp.where(up, r0, l1)
            + far * jnp.where(up, l0, r1)
        )

    def meridional(field):
        def column(i, _):
            l, y = i // 4, lanes(i % 4)
            q = [field[l, j, :, y] for j in range(14)]
            d = [None] + [q[j] - q[j - 1] for j in range(1, 14)]
            e = {f: edge_dev(d[f - 1], d[f], d[f + 1]) for f in range(2, 13)}
            dev = {j: limited(e[j] - d[j], e[j + 1]) for j in range(2, 12)}
            across = []
            for f in range(3, 12):
                r = pl.ds(f - 3, 1)
                terms = [wide(c_mer, k, l, r, y) for k in range(3)]
                (l0, r0), (l1, r1) = dev[f - 1], dev[f]
                across.append(flux(*terms, q[f - 1], r0, l0, q[f], l1, r1))
            for r in range(ROWS):
                kept, inv = (wide(w_mer, k, l, pl.ds(r, 1), y) for k in range(2))
                mid[l, r, :, y] = kept * q[r + 3] + inv * (across[r] - across[r + 1])
            return 0

        lax.fori_loop(0, LEV * 4, column, 0)

    lane = lax.broadcasted_iota(jnp.int32, (TRC, BLK), 1)

    def shifted(tiles, by):
        turned = [pltpu.roll(tile, -by % BLK, axis=1) for tile in tiles]
        inside = lane < BLK - by if by > 0 else lane >= -by
        step = 1 if by > 0 else -1
        return [jnp.where(inside, turned[b], turned[(b + step) % 4]) for b in range(4)]

    def zonal_row(r):
        at = pl.ds(r, 1)
        for l in range(LEV):
            q = [mid[l, r, :, b * BLK : (b + 1) * BLK] for b in range(4)]
            west2, west, east, east2 = (shifted(q, by) for by in (-2, -1, 1, 2))
            out_east, out_west = [], []
            for b in range(4):
                d_w, d, d_e, d_ee = west[b] - west2[b], q[b] - west[b], east[b] - q[b], east2[b] - east[b]
                left, right = limited(edge_dev(d_w, d, d_e) - d, edge_dev(d, d_e, d_ee))
                v0, n0, f0, v1, n1, f1 = (wide(c_zon, k, l, at, pl.ds(b * BLK, BLK)) for k in range(6))
                out_east.append(v0 * q[b] + n0 * right + f0 * left)
                out_west.append(v1 * q[b] + n1 * left + f1 * right)
            from_west, from_east = shifted(out_east, -1), shifted(out_west, 1)
            for b in range(4):
                y = pl.ds(b * BLK, BLK)
                kept, inv = (wide(w_zon, k, l, at, y) for k in range(2))
                gain = (from_west[b] - out_east[b]) + (out_west[b] - from_east[b])
                mid2[l, :, y] = kept * q[b] + inv * gain

    def vertical_row(r, target, offset):
        def block(b, _):
            y, at = lanes(b), pl.ds(r, 1)
            q = [mid2[l, :, y] for l in range(LEV)]
            none = jnp.zeros((TRC, BLK), F32)
            d = [none] + [q[l] - q[l - 1] for l in range(1, LEV)] + [none]
            e = [none] + [edge_dev(d[f - 1], d[f], d[f + 1]) for f in range(1, LEV)] + [none]
            dev = [(none, none)] + [limited(e[l] - d[l], e[l + 1]) for l in range(1, LEV - 1)] + [(none, none)]
            across = [None]
            for f in range(1, LEV):
                terms = [wide(c_ver, k, f - 1, at, y) for k in range(3)]
                (l0, r0), (l1, r1) = dev[f - 1], dev[f]
                across.append(flux(*terms, q[f - 1], r0, l0, q[f], l1, r1))
            across.append(wide(c_ver, 0, LEV - 1, at, y) * q[LEV - 1])
            share = rate * jnp.broadcast_to(sea_f[at, y], (TRC, BLK))
            for l in range(LEV):
                kept, inv = (wide(w_ver, k, l, at, y) for k in range(2))
                gain = -across[l + 1] if l == 0 else across[l] - across[l + 1]
                new = kept * q[l] + inv * gain
                other = jnp.take_along_axis(new, partner, axis=0)
                target[l, offset + r, :, y] = new + share * (other - new)
            return 0

        lax.fori_loop(0, 4, block, 0)

    sea_f = depth.at[LEV]
    sea_f[...] = sea

    def run_rows(first, last, target, offset):
        for r in range(first, last):
            zonal_row(r)
            vertical_row(r, target, offset)

    for sem in (1, 2, 3):
        arrived(sem)
    mer_terms(0)
    for copy in halos:
        copy.wait()
    clear_ends(field_a)
    meridional(field_a)
    gather_y(2)
    gather_y(3)
    arrived(15)
    zon_terms(0)
    ver_terms(0)
    halos = field_halos(field_b, 10)
    run_rows(0, 3, field_b, 3)
    halos[1].start()
    run_rows(5, 8, field_b, 3)
    halos[0].start()
    run_rows(3, 5, field_b, 3)

    arrived(19)
    mer_terms(1)
    for copy in halos:
        copy.wait()
    clear_ends(field_b)
    meridional(field_b)
    arrived(23)
    zon_terms(1)
    ver_terms(1)
    stores = []
    for half in range(2):
        run_rows(4 * half, 4 * half + 4, done, 0)
        part_of = pl.ds(4 * half, 4)
        for t in range(TRC):
            sem = local_sem.at[36 + 8 * half + t]
            stores.append(pltpu.make_async_copy(done.at[:, part_of, t], out.at[t, :, part_of], sem))
            stores[-1].start()
    for sem, like in likes.items():
        all_bytes(send_sem.at[sem], like)
    for copy in rows:
        copy.wait_send()
    for copy in stores:
        copy.wait()


def per_device(*args):
    any_space = pl.BlockSpec(memory_space=pl.ANY)
    vmem = pltpu.VMEM
    return pl.pallas_call(
        kernel,
        out_shape=jax.ShapeDtypeStruct((TRC, LEV, ROWS, LON), F32),
        in_specs=[any_space] * 7,
        out_specs=any_space,
        scratch_shapes=[
            vmem((4, RING, 2, ROWS, BLK), F32),
            vmem((RING, 2, ROWS, BLK), F32),
            *[vmem((4, 4, 2, ROWS, BLK), F32)] * 3,
            vmem((4, 4, 2, ROWS, BLK), F32),
            *[vmem((4, 2, ROWS, BLK), F32)] * 2,
            *[vmem((4, 2, ROWS, BLK), F32)] * 3,
            vmem((4, 3, ROWS, BLK), F32),
            *[vmem((4, 2, ROWS, BLK), F32)] * 2,
            vmem((2, ROWS, BLK), F32),
            *[vmem((ROWS, BLK), F32)] * STEPS,
            vmem((STEPS, LEV, 3, ROWS, LON), F32),
            vmem((STEPS, LEV, 2, ROWS, LON), F32),
            vmem((ROWS, LON), jnp.int32),
            vmem((ROWS, LON), jnp.int32),
            vmem((LEV, 14, TRC, LON), F32),
            vmem((LEV, 14, TRC, LON), F32),
            vmem((LEV, ROWS, TRC, LON), F32),
            vmem((LEV, TRC, LON), F32),
            vmem((LEV, ROWS, TRC, LON), F32),
            vmem((3, LEV, 2 * ROWS, LON), F32),
            vmem((6, LEV, ROWS, LON), F32),
            vmem((3, LEV, ROWS, LON), F32),
            vmem((2, LEV, ROWS, LON), F32),
            vmem((2, LEV, ROWS, LON), F32),
            vmem((2, LEV, ROWS, LON), F32),
            vmem((LEV + 1, ROWS, LON), F32),
            pltpu.SMEM((STEPS,), jnp.int32),
            pltpu.SMEM((TRC,), jnp.int32),
            pltpu.SMEM((TRC,), F32),
            pltpu.SemaphoreType.DMA((52,)),
            pltpu.SemaphoreType.DMA((24,)),
            pltpu.SemaphoreType.DMA((24,)),
        ],
        compiler_params=pltpu.CompilerParams(
            collective_id=0, has_side_effects=True, vmem_limit_bytes=60 * 1024 * 1024
        ),
    )(*args)


def solution(mesh):
    placed = (
        P("trc", None, "lat", None),
        P(None, "trc", None, None, "lat", None),
        P(None, "trc", None, "lat", None),
        P(),
        P("lat", None),
        P("trc"),
        P("trc"),
    )
    return jax.shard_map(
        per_device,
        mesh=mesh,
        in_specs=placed,
        out_specs=P("trc", None, "lat", None),
        check_vma=False,
    )
```

```python
import functools

import jax
import jax.numpy as jnp
from jax import lax
from jax.experimental import pallas as pl
from jax.experimental.pallas import tpu as pltpu
from jax.sharding import PartitionSpec as P

MESH = pl.DeviceIdType.MESH
TRC, LEV, ROWS, LON, STEPS, RING = 8, 4, 8, 512, 2, 16
BLK = 128
F32 = jnp.float32

GROUPS = (((0, 1), (0, -1)), ((0, 0), (0, 2)), ((1, 1), (1, -1)), ((1, 0), (1, 2)))


def limited(left, right):
    two_l, two_r = 2.0 * jnp.abs(left), 2.0 * jnp.abs(right)
    return (
        jnp.minimum(jnp.maximum(left, -two_r), two_r),
        jnp.minimum(jnp.maximum(right, -two_l), two_l),
    )


def edge_dev(before, here, after):
    dev = 0.5 * here + (1.0 / 12.0) * (before - after)
    return jnp.minimum(jnp.maximum(dev, jnp.minimum(here, 0.0)), jnp.maximum(here, 0.0))


def face_terms(flow, depth_up):
    courant = jnp.abs(flow) / jnp.maximum(depth_up, 0.25)
    rest = 1.0 - courant
    scaled = flow * rest
    return scaled * rest, -courant * scaled


def kernel(
    tracers, transports, thickness, owner, land_sea, pairs, rates, out,
    stage, along_y0, along_y1, along_y2, along_y3, along_z0, along_z1, along_z2, along_z3,
    quarter0, quarter1, quarter2, quarter3, part0, part1, part2, part3, border0, border1, rec_a, rec_b, sea_int, sea_halo_int,
    field_a, field_b, dev_l, dev_r, mid, mid2, done,
    c_mer, c_zon, c_ver, w_mer, w_zon, w_ver, depth,
    owner_s, pairs_s, rates_s,
    local_sem, send_sem, recv_sem,
):
    along_y, along_z = (along_y0, along_y1, along_y2, along_y3), (along_z0, along_z1, along_z2, along_z3)
    quarter, part = (quarter0, quarter1, quarter2, quarter3), (part0, part1, part2, part3)
    border = (border0, None, border1)
    lat, me = lax.axis_index("lat"), lax.axis_index("trc")
    my_y, my_z = me // 4, me % 4
    north, south = lax.rem(lat + 1, RING), lax.rem(lat + RING - 1, RING)

    def lanes(y):
        return pl.ds(pl.multiple_of(y * BLK, BLK), BLK)

    barrier = pltpu.get_barrier_semaphore()

    for beside in (north, south):
        pl.semaphore_signal(barrier, inc=1, device_id={"lat": beside}, device_id_type=MESH)
    for k in range(1, 4):
        for peer in (my_y * 4 + lax.rem(my_z + k, 4), lax.rem(my_y + k, 4) * 4 + my_z):
            pl.semaphore_signal(barrier, inc=1, device_id={"trc": peer}, device_id_type=MESH)

    stages = []
    for g, fields in enumerate(GROUPS):
        copies = []
        for f, (s, k) in enumerate(fields):
            source = thickness.at[s, 0] if k < 0 else transports.at[s, 0, k]
            for y in range(4):
                copies.append(
                    pltpu.make_async_copy(
                        source.at[:, :, pl.ds(y * BLK, BLK)],
                        stage.at[g, pl.ds(4 * y, 4), f],
                        local_sem.at[8 * g + 4 * f + y],
                    )
                )
        for copy in copies:
            copy.start()
        stages.append(copies)
    smalls = [
        pltpu.make_async_copy(owner, owner_s, local_sem.at[32]),
        pltpu.make_async_copy(pairs, pairs_s, local_sem.at[33]),
        pltpu.make_async_copy(rates, rates_s, local_sem.at[34]),
        pltpu.make_async_copy(land_sea, sea_int, local_sem.at[35]),
    ]
    loads = [
        pltpu.make_async_copy(
            tracers.at[t], field_a.at[:, pl.ds(3, ROWS), t], local_sem.at[36 + t]
        )
        for t in range(TRC)
    ]
    for copy in smalls + loads:
        copy.start()

    pl.semaphore_wait(barrier, 8)

    def one_copy(source, target, sem, **where):
        return pltpu.make_async_remote_copy(
            source, target, send_sem.at[sem], recv_sem.at[sem], device_id=where, device_id_type=MESH
        )

    def along(axis, source, target, sem):
        for k in (2, 1, 3):
            if axis == "y":
                at = lax.rem(my_y + k, 4)
                one_copy(source(at), target, sem, trc=at * 4 + my_z).start()
            else:
                at = lax.rem(my_z + k, 4)
                one_copy(source(at), target, sem, trc=my_y * 4 + at).start()

    def all_bytes(sems, like):
        pltpu.make_async_copy(like, like, sems).wait()

    for_north, for_south = pl.ds(0, 1), pl.ds(1, 2)

    def put_border(rows, tile):
        rows[0:1], rows[1:2], rows[2:3] = tile[1, 7:8], tile[1, 0:1], tile[0, 0:1]

    three = pl.ds(0, 3)
    likes = {s + 2 * i: rec_a.at[s, :, 2, rows] for s in range(STEPS) for i, rows in enumerate((for_north, for_south))}
    for g in range(4):
        for k in range(3):
            likes[12 + 3 * g + k] = along_y[g].at[three]

    def arrived(sem):
        all_bytes(recv_sem.at[sem], likes[sem])

    def scatter_y(g):
        for copy in stages[g]:
            copy.wait()
        along("y", lambda y: stage.at[g, pl.ds(4 * y, 4)], along_y[g].at[my_y], 12 + 3 * g)
        along_y[g][my_y] = stage[g, pl.ds(4 * my_y, 4)]

    def spread_z(g):
        arrived(12 + 3 * g)
        quarter[g][...] = along_y[g][owner_s[g // 2] // 4]
        along("z", lambda z: quarter[g], along_z[g].at[my_z], 13 + 3 * g)
        along_z[g][my_z] = quarter[g][...]

    def gather_y(g):
        arrived(13 + 3 * g)
        part[g][...] = along_z[g][lax.rem(owner_s[g // 2], 4)]
        s, first = g // 2, g % 2 == 0
        rec = (rec_a if first else rec_b).at[s, :, pl.ds(0, 2), :, lanes(my_y)]
        along("y", lambda y: part[g], rec, 14 + 3 * g)
        if first:
            for l in range(LEV):
                put_border(border[g].at[l], part[g][l])
            for k in (2, 1, 3, 0):
                there = lax.rem(my_y + k, 4) * 4 + my_z
                for part_of, sem, where in ((for_north, s, north), (for_south, s + 2, south)):
                    target = rec_a.at[s, :, 2, part_of, lanes(my_y)]
                    one_copy(border[g].at[:, part_of], target, sem, lat=where, trc=there).start()
        rec[...] = part[g][...]

    for g in range(4):
        scatter_y(g)
    rows = [
        one_copy(land_sea.at[pl.ds(7, 1)], sea_halo_int.at[pl.ds(0, 1)], 6, lat=north),
        one_copy(land_sea.at[pl.ds(0, 1)], sea_halo_int.at[pl.ds(1, 1)], 7, lat=south),
    ]
    for copy in rows:
        copy.start()
    for copy in smalls:
        copy.wait()
    spread_z(0)
    spread_z(1)

    def field_halos(field, sem):
        return [
            one_copy(field.at[:, pl.ds(8, 3)], field.at[:, pl.ds(0, 3)], sem, lat=north),
            one_copy(field.at[:, pl.ds(3, 3)], field.at[:, pl.ds(11, 3)], sem + 1, lat=south),
        ]

    def clear_south(field):
        @pl.when(lat == 0)
        def _():
            field[:, 0:3] = jnp.zeros((LEV, 3, TRC, LON), F32)

    def clear_north(field):
        @pl.when(lat == RING - 1)
        def _():
            field[:, 11:14] = jnp.zeros((LEV, 3, TRC, LON), F32)

    for copy in loads:
        copy.wait()
    halos = field_halos(field_a, 8)
    for copy in halos:
        copy.start()

    spread_z(2)
    spread_z(3)

    for copy in rows:
        copy.wait_recv()
    sub = lax.broadcasted_iota(jnp.int32, (ROWS, LON), 0)
    sea = sea_int[...].astype(F32)
    sea_s = jnp.where(lat > 0, sea_halo_int[0:1].astype(F32), 0.0)
    sea_n = jnp.where(lat < RING - 1, sea_halo_int[1:2].astype(F32), 0.0)
    mask_mer = sea * jnp.where(sub == 0, sea_s, pltpu.roll(sea, 1, axis=0))
    mask_top = sea[7:8] * sea_n
    mask_zon = sea * pltpu.roll(sea, LON - 1, axis=1)
    sub1 = lax.broadcasted_iota(jnp.int32, (TRC, BLK), 0)
    partner = jnp.zeros((TRC, BLK), jnp.int32)
    rate = jnp.zeros((TRC, BLK), F32)
    for i in range(TRC):
        partner = jnp.where(sub1 == i, pairs_s[i] - me * TRC, partner)
        rate = jnp.where(sub1 == i, rates_s[i], rate)

    def mer_terms(s):
        def level(l, _):
            flow0, h, x = rec_a[s, l, 0], rec_a[s, l, 1], rec_a[s, l, 2]
            flow = flow0 * mask_mer
            below = jnp.where(sub == 0, x[0:1], pltpu.roll(h, 1, axis=0))
            near, far = face_terms(flow, jnp.where(flow > 0, below, h))
            c_mer[0, l, 0:8], c_mer[1, l, 0:8], c_mer[2, l, 0:8] = flow, near, far
            top = x[2:3] * mask_top
            near, far = face_terms(top, jnp.where(top > 0, h[7:8], x[1:2]))
            c_mer[0, l, 8:9], c_mer[1, l, 8:9], c_mer[2, l, 8:9] = top, near, far
            h_new = h + flow - jnp.where(sub == 7, top, pltpu.roll(flow, 7, axis=0))
            inv = 1.0 / h_new
            w_mer[0, l], w_mer[1, l] = h * inv, inv
            depth[l] = h_new
            return 0

        lax.fori_loop(0, LEV, level, 0)

    def zon_terms(s):
        def level(l, _):
            h = depth[l]
            east = rec_b[s, l, 0] * mask_zon
            west = pltpu.roll(east, 1, axis=1)
            h_new = h + west - east
            inv = 1.0 / h_new
            flow = jnp.maximum(east, 0.0)
            c_zon[0, l] = flow
            c_zon[1, l], c_zon[2, l] = face_terms(flow, h)
            flow = jnp.minimum(west, 0.0)
            c_zon[3, l] = flow
            c_zon[4, l], c_zon[5, l] = face_terms(flow, h)
            w_zon[0, l], w_zon[1, l] = h * inv, inv
            depth[l] = h_new
            return 0

        lax.fori_loop(0, LEV, level, 0)

    def ver_terms(s):
        flow_in = jnp.zeros((ROWS, LON), F32)
        for l in range(LEV):
            h = depth[l]
            flow = rec_b[s, l, 1] * sea
            c_ver[0, l] = flow
            if l < LEV - 1:
                c_ver[1, l], c_ver[2, l] = face_terms(flow, jnp.where(flow > 0, h, depth[l + 1]))
            inv = 1.0 / (h + flow_in - flow)
            w_ver[0, l], w_ver[1, l] = h * inv, inv
            flow_in = flow

    def wide(ref, *at):
        return jnp.broadcast_to(ref[at], (TRC, ref[at].shape[-1]))

    def flux(flow, near, far, q0, r0, l0, q1, l1, r1):
        up = flow > 0
        return (
            flow * jnp.where(up, q0, q1)
            + near * jnp.where(up, r0, l1)
            + far * jnp.where(up, l0, r1)
        )

    def columns(body):
        def column(i, _):
            body(i // 4, lanes(i % 4))
            return 0

        lax.fori_loop(0, LEV * 4, column, 0)

    def reconstruct(field, first, last):
        def body(l, y):
            q = {j: field[l, j, :, y] for j in range(first - 2, last + 2)}
            d = {f: q[f] - q[f - 1] for f in range(first - 1, last + 2)}
            e = {f: edge_dev(d[f - 1], d[f], d[f + 1]) for f in range(first, last + 1)}
            for j in range(first, last):
                dev_l[l, j, :, y], dev_r[l, j, :, y] = limited(e[j] - d[j], e[j + 1])

        columns(body)

    def meridional(field, first, last):
        def body(l, y):
            q = {j: field[l, j, :, y] for j in range(first + 2, last + 4)}
            dev = {j: (dev_l[l, j, :, y], dev_r[l, j, :, y]) for j in range(first + 2, last + 4)}
            across = {}
            for f in range(first + 3, last + 4):
                terms = [wide(c_mer, k, l, pl.ds(f - 3, 1), y) for k in range(3)]
                (l0, r0), (l1, r1) = dev[f - 1], dev[f]
                across[f] = flux(*terms, q[f - 1], r0, l0, q[f], l1, r1)
            for r in range(first, last):
                kept, inv = (wide(w_mer, k, l, pl.ds(r, 1), y) for k in range(2))
                mid[l, r, :, y] = kept * q[r + 3] + inv * (across[r + 3] - across[r + 4])

        columns(body)

    lane = lax.broadcasted_iota(jnp.int32, (TRC, BLK), 1)

    def shifted(tiles, by):
        turned = [pltpu.roll(tile, -by % BLK, axis=1) for tile in tiles]
        inside = lane < BLK - by if by > 0 else lane >= -by
        step = 1 if by > 0 else -1
        return [jnp.where(inside, turned[b], turned[(b + step) % 4]) for b in range(4)]

    def zonal_row(r):
        at = pl.ds(r, 1)
        for l in range(LEV):
            q = [mid[l, r, :, b * BLK : (b + 1) * BLK] for b in range(4)]
            west2, west, east, east2 = (shifted(q, by) for by in (-2, -1, 1, 2))
            out_east, out_west = [], []
            for b in range(4):
                d_w, d, d_e, d_ee = west[b] - west2[b], q[b] - west[b], east[b] - q[b], east2[b] - east[b]
                left, right = limited(edge_dev(d_w, d, d_e) - d, edge_dev(d, d_e, d_ee))
                v0, n0, f0, v1, n1, f1 = (wide(c_zon, k, l, at, pl.ds(b * BLK, BLK)) for k in range(6))
                out_east.append(v0 * q[b] + n0 * right + f0 * left)
                out_west.append(v1 * q[b] + n1 * left + f1 * right)
            from_west, from_east = shifted(out_east, -1), shifted(out_west, 1)
            for b in range(4):
                y = pl.ds(b * BLK, BLK)
                kept, inv = (wide(w_zon, k, l, at, y) for k in range(2))
                gain = (from_west[b] - out_east[b]) + (out_west[b] - from_east[b])
                mid2[l, :, y] = kept * q[b] + inv * gain

    def vertical_row(r, target, offset):
        def block(b, _):
            y, at = lanes(b), pl.ds(r, 1)
            q = [mid2[l, :, y] for l in range(LEV)]
            none = jnp.zeros((TRC, BLK), F32)
            d = [none] + [q[l] - q[l - 1] for l in range(1, LEV)] + [none]
            e = [none] + [edge_dev(d[f - 1], d[f], d[f + 1]) for f in range(1, LEV)] + [none]
            dev = [(none, none)] + [limited(e[l] - d[l], e[l + 1]) for l in range(1, LEV - 1)] + [(none, none)]
            across = [None]
            for f in range(1, LEV):
                terms = [wide(c_ver, k, f - 1, at, y) for k in range(3)]
                (l0, r0), (l1, r1) = dev[f - 1], dev[f]
                across.append(flux(*terms, q[f - 1], r0, l0, q[f], l1, r1))
            across.append(wide(c_ver, 0, LEV - 1, at, y) * q[LEV - 1])
            share = rate * jnp.broadcast_to(sea_f[at, y], (TRC, BLK))
            for l in range(LEV):
                kept, inv = (wide(w_ver, k, l, at, y) for k in range(2))
                gain = -across[l + 1] if l == 0 else across[l] - across[l + 1]
                new = kept * q[l] + inv * gain
                other = jnp.take_along_axis(new, partner, axis=0)
                target[l, offset + r, :, y] = new + share * (other - new)
            return 0

        lax.fori_loop(0, 4, block, 0)

    sea_f = depth.at[LEV]
    sea_f[...] = sea

    def run_rows(first, last, target, offset):
        for r in range(first, last):
            zonal_row(r)
            vertical_row(r, target, offset)

    gather_y(0)
    for copy in halos:
        copy.wait_recv()
    clear_south(field_a)
    clear_north(field_a)
    reconstruct(field_a, 2, 12)
    gather_y(1)
    for sem in (14, 0, 2):
        arrived(sem)
    mer_terms(0)
    meridional(field_a, 0, ROWS)
    gather_y(2)
    arrived(17)
    zon_terms(0)
    ver_terms(0)
    next_halos = field_halos(field_b, 10)
    run_rows(0, 3, field_b, 3)
    next_halos[1].start()
    gather_y(3)
    run_rows(5, 8, field_b, 3)
    next_halos[0].start()
    run_rows(3, 5, field_b, 3)

    reconstruct(field_b, 5, 9)
    for sem in (20, 1, 3):
        arrived(sem)
    mer_terms(1)
    next_halos[1].wait_recv()
    clear_north(field_b)
    reconstruct(field_b, 9, 12)
    meridional(field_b, 3, ROWS)
    arrived(23)
    zon_terms(1)
    ver_terms(1)
    stores = []

    def finish(first, last):
        run_rows(first, last, done, 0)
        part_of = pl.ds(first, last - first)
        for t in range(TRC):
            sem = local_sem.at[36 + len(stores)]
            stores.append(pltpu.make_async_copy(done.at[:, part_of, t], out.at[t, :, part_of], sem))
            stores[-1].start()

    finish(3, ROWS)
    next_halos[0].wait_recv()
    clear_south(field_b)
    reconstruct(field_b, 2, 5)
    meridional(field_b, 0, 3)
    finish(0, 3)
    for copy in halos + next_halos:
        copy.wait_send()
    for sem, like in likes.items():
        all_bytes(send_sem.at[sem], like)
    for copy in rows:
        copy.wait_send()
    for copy in stores:
        copy.wait()


def per_device(*args):
    any_space = pl.BlockSpec(memory_space=pl.ANY)
    vmem = pltpu.VMEM
    return pl.pallas_call(
        kernel,
        out_shape=jax.ShapeDtypeStruct((TRC, LEV, ROWS, LON), F32),
        in_specs=[any_space] * 7,
        out_specs=any_space,
        scratch_shapes=[
            vmem((4, RING, 2, ROWS, BLK), F32),
            *[vmem((4, 4, 2, ROWS, BLK), F32)] * 4,
            *[vmem((4, 4, 2, ROWS, BLK), F32)] * 4,
            *[vmem((4, 2, ROWS, BLK), F32)] * 4,
            *[vmem((4, 2, ROWS, BLK), F32)] * 4,
            *[vmem((LEV, ROWS, BLK), F32)] * STEPS,
            vmem((STEPS, LEV, 3, ROWS, LON), F32),
            vmem((STEPS, LEV, 2, ROWS, LON), F32),
            vmem((ROWS, LON), jnp.int32),
            vmem((ROWS, LON), jnp.int32),
            vmem((LEV, 14, TRC, LON), F32),
            vmem((LEV, 14, TRC, LON), F32),
            vmem((LEV, 14, TRC, LON), F32),
            vmem((LEV, 14, TRC, LON), F32),
            vmem((LEV, ROWS, TRC, LON), F32),
            vmem((LEV, TRC, LON), F32),
            vmem((LEV, ROWS, TRC, LON), F32),
            vmem((3, LEV, 2 * ROWS, LON), F32),
            vmem((6, LEV, ROWS, LON), F32),
            vmem((3, LEV, ROWS, LON), F32),
            vmem((2, LEV, ROWS, LON), F32),
            vmem((2, LEV, ROWS, LON), F32),
            vmem((2, LEV, ROWS, LON), F32),
            vmem((LEV + 1, ROWS, LON), F32),
            pltpu.SMEM((STEPS,), jnp.int32),
            pltpu.SMEM((TRC,), jnp.int32),
            pltpu.SMEM((TRC,), F32),
            pltpu.SemaphoreType.DMA((52,)),
            pltpu.SemaphoreType.DMA((24,)),
            pltpu.SemaphoreType.DMA((24,)),
        ],
        compiler_params=pltpu.CompilerParams(
            collective_id=0, has_side_effects=True, vmem_limit_bytes=60 * 1024 * 1024
        ),
    )(*args)


def solution(mesh):
    placed = (
        P("trc", None, "lat", None),
        P(None, "trc", None, None, "lat", None),
        P(None, "trc", None, "lat", None),
        P(),
        P("lat", None),
        P("trc"),
        P("trc"),
    )
    return jax.shard_map(
        per_device,
        mesh=mesh,
        in_specs=placed,
        out_specs=P("trc", None, "lat", None),
        check_vma=False,
    )
```

```python
import functools

import jax
import jax.numpy as jnp
from jax import lax
from jax.experimental import pallas as pl
from jax.experimental.pallas import tpu as pltpu
from jax.sharding import PartitionSpec as P

MESH = pl.DeviceIdType.MESH
TRC, LEV, ROWS, LON, STEPS, RING = 8, 4, 8, 512, 2, 16
BLK = 128
F32 = jnp.float32

GROUPS = (((0, 1), (0, -1)), ((0, 0), (0, 2)), ((1, 1), (1, -1)), ((1, 0), (1, 2)))


def limited(left, right):
    two_l, two_r = 2.0 * jnp.abs(left), 2.0 * jnp.abs(right)
    return (
        jnp.minimum(jnp.maximum(left, -two_r), two_r),
        jnp.minimum(jnp.maximum(right, -two_l), two_l),
    )


def edge_dev(before, here, after):
    dev = 0.5 * here + (1.0 / 12.0) * (before - after)
    return jnp.minimum(jnp.maximum(dev, jnp.minimum(here, 0.0)), jnp.maximum(here, 0.0))


def face_terms(flow, depth_up):
    courant = jnp.abs(flow) / jnp.maximum(depth_up, 0.25)
    rest = 1.0 - courant
    scaled = flow * rest
    return scaled * rest, -courant * scaled


def kernel(
    tracers, transports, thickness, owner, land_sea, pairs, rates, out,
    stage, along_y0, along_y1, along_y2, along_y3, along_z0, along_z1, along_z2, along_z3,
    quarter0, quarter1, quarter2, quarter3, part0, part1, part2, part3, border0, border1, rec_a, rec_b, sea_int, sea_halo_int,
    field_a, field_b, dev_l, dev_r, mid, mid2, done,
    c_mer, c_zon, c_ver, w_mer, w_zon, w_ver, depth,
    owner_s, pairs_s, rates_s,
    local_sem, send_sem, recv_sem,
):
    along_y, along_z = (along_y0, along_y1, along_y2, along_y3), (along_z0, along_z1, along_z2, along_z3)
    quarter, part = (quarter0, quarter1, quarter2, quarter3), (part0, part1, part2, part3)
    border = (border0, None, border1)
    lat, me = lax.axis_index("lat"), lax.axis_index("trc")
    my_y, my_z = me // 4, me % 4
    north, south = lax.rem(lat + 1, RING), lax.rem(lat + RING - 1, RING)

    def lanes(y):
        return pl.ds(pl.multiple_of(y * BLK, BLK), BLK)

    barrier = pltpu.get_barrier_semaphore()

    for beside in (north, south):
        pl.semaphore_signal(barrier, inc=1, device_id={"lat": beside}, device_id_type=MESH)
    for k in range(1, 4):
        for peer in (my_y * 4 + lax.rem(my_z + k, 4), lax.rem(my_y + k, 4) * 4 + my_z):
            pl.semaphore_signal(barrier, inc=1, device_id={"trc": peer}, device_id_type=MESH)

    stages = []
    for g, fields in enumerate(GROUPS):
        copies = []
        for f, (s, k) in enumerate(fields):
            source = thickness.at[s, 0] if k < 0 else transports.at[s, 0, k]
            for y in range(4):
                copies.append(
                    pltpu.make_async_copy(
                        source.at[:, :, pl.ds(y * BLK, BLK)],
                        stage.at[g, pl.ds(4 * y, 4), f],
                        local_sem.at[8 * g + 4 * f + y],
                    )
                )
        for copy in copies:
            copy.start()
        stages.append(copies)
    smalls = [
        pltpu.make_async_copy(owner, owner_s, local_sem.at[32]),
        pltpu.make_async_copy(pairs, pairs_s, local_sem.at[33]),
        pltpu.make_async_copy(rates, rates_s, local_sem.at[34]),
        pltpu.make_async_copy(land_sea, sea_int, local_sem.at[35]),
    ]
    loads = [
        pltpu.make_async_copy(
            tracers.at[t], field_a.at[:, pl.ds(3, ROWS), t], local_sem.at[36 + t]
        )
        for t in range(TRC)
    ]
    for copy in smalls + loads:
        copy.start()

    pl.semaphore_wait(barrier, 8)

    def one_copy(source, target, sem, **where):
        return pltpu.make_async_remote_copy(
            source, target, send_sem.at[sem], recv_sem.at[sem], device_id=where, device_id_type=MESH
        )

    def along(axis, source, target, sem):
        for k in (2, 1, 3):
            if axis == "y":
                at = lax.rem(my_y + k, 4)
                one_copy(source(at), target, sem, trc=at * 4 + my_z).start()
            else:
                at = lax.rem(my_z + k, 4)
                one_copy(source(at), target, sem, trc=my_y * 4 + at).start()

    def all_bytes(sems, like):
        pltpu.make_async_copy(like, like, sems).wait()

    for_north, for_south = pl.ds(0, 1), pl.ds(1, 2)

    def put_border(rows, tile):
        rows[0:1], rows[1:2], rows[2:3] = tile[1, 7:8], tile[1, 0:1], tile[0, 0:1]

    three = pl.ds(0, 3)
    likes = {s + 2 * i: rec_a.at[s, :, 2, rows] for s in range(STEPS) for i, rows in enumerate((for_north, for_south))}
    for g in range(4):
        for k in range(3):
            likes[12 + 3 * g + k] = along_y[g].at[three]

    def arrived(sem):
        all_bytes(recv_sem.at[sem], likes[sem])

    def scatter_y(g):
        for copy in stages[g]:
            copy.wait()
        along("y", lambda y: stage.at[g, pl.ds(4 * y, 4)], along_y[g].at[my_y], 12 + 3 * g)
        along_y[g][my_y] = stage[g, pl.ds(4 * my_y, 4)]

    def spread_z(g):
        arrived(12 + 3 * g)
        quarter[g][...] = along_y[g][owner_s[g // 2] // 4]
        along("z", lambda z: quarter[g], along_z[g].at[my_z], 13 + 3 * g)
        along_z[g][my_z] = quarter[g][...]

    def gather_y(g):
        arrived(13 + 3 * g)
        part[g][...] = along_z[g][lax.rem(owner_s[g // 2], 4)]
        s, first = g // 2, g % 2 == 0
        rec = (rec_a if first else rec_b).at[s, :, pl.ds(0, 2), :, lanes(my_y)]
        along("y", lambda y: part[g], rec, 14 + 3 * g)
        if first:
            for l in range(LEV):
                put_border(border[g].at[l], part[g][l])
            for k in (2, 1, 3, 0):
                there = lax.rem(my_y + k, 4) * 4 + my_z
                for part_of, sem, where in ((for_north, s, north), (for_south, s + 2, south)):
                    target = rec_a.at[s, :, 2, part_of, lanes(my_y)]
                    one_copy(border[g].at[:, part_of], target, sem, lat=where, trc=there).start()
        rec[...] = part[g][...]

    def field_halos(field, sem):
        return [
            one_copy(field.at[:, pl.ds(8, 3)], field.at[:, pl.ds(0, 3)], sem, lat=north),
            one_copy(field.at[:, pl.ds(3, 3)], field.at[:, pl.ds(11, 3)], sem + 1, lat=south),
        ]

    def clear_south(field):
        @pl.when(lat == 0)
        def _():
            field[:, 0:3] = jnp.zeros((LEV, 3, TRC, LON), F32)

    def clear_north(field):
        @pl.when(lat == RING - 1)
        def _():
            field[:, 11:14] = jnp.zeros((LEV, 3, TRC, LON), F32)

    for copy in loads:
        copy.wait()
    halos = field_halos(field_a, 8)
    for copy in halos:
        copy.start()

    for g in range(4):
        scatter_y(g)
    rows = [
        one_copy(land_sea.at[pl.ds(7, 1)], sea_halo_int.at[pl.ds(0, 1)], 6, lat=north),
        one_copy(land_sea.at[pl.ds(0, 1)], sea_halo_int.at[pl.ds(1, 1)], 7, lat=south),
    ]
    for copy in rows:
        copy.start()
    for copy in smalls:
        copy.wait()
    spread_z(0)
    spread_z(1)


    for copy in rows:
        copy.wait_recv()
    sub = lax.broadcasted_iota(jnp.int32, (ROWS, LON), 0)
    sea = sea_int[...].astype(F32)
    sea_s = jnp.where(lat > 0, sea_halo_int[0:1].astype(F32), 0.0)
    sea_n = jnp.where(lat < RING - 1, sea_halo_int[1:2].astype(F32), 0.0)
    mask_mer = sea * jnp.where(sub == 0, sea_s, pltpu.roll(sea, 1, axis=0))
    mask_top = sea[7:8] * sea_n
    mask_zon = sea * pltpu.roll(sea, LON - 1, axis=1)
    sub1 = lax.broadcasted_iota(jnp.int32, (TRC, BLK), 0)
    partner = jnp.zeros((TRC, BLK), jnp.int32)
    rate = jnp.zeros((TRC, BLK), F32)
    for i in range(TRC):
        partner = jnp.where(sub1 == i, pairs_s[i] - me * TRC, partner)
        rate = jnp.where(sub1 == i, rates_s[i], rate)

    def mer_terms(s):
        def level(l, _):
            flow0, h, x = rec_a[s, l, 0], rec_a[s, l, 1], rec_a[s, l, 2]
            flow = flow0 * mask_mer
            below = jnp.where(sub == 0, x[0:1], pltpu.roll(h, 1, axis=0))
            near, far = face_terms(flow, jnp.where(flow > 0, below, h))
            c_mer[0, l, 0:8], c_mer[1, l, 0:8], c_mer[2, l, 0:8] = flow, near, far
            top = x[2:3] * mask_top
            near, far = face_terms(top, jnp.where(top > 0, h[7:8], x[1:2]))
            c_mer[0, l, 8:9], c_mer[1, l, 8:9], c_mer[2, l, 8:9] = top, near, far
            h_new = h + flow - jnp.where(sub == 7, top, pltpu.roll(flow, 7, axis=0))
            inv = 1.0 / h_new
            w_mer[0, l], w_mer[1, l] = h * inv, inv
            depth[l] = h_new
            return 0

        lax.fori_loop(0, LEV, level, 0)

    def zon_terms(s):
        def level(l, _):
            h = depth[l]
            east = rec_b[s, l, 0] * mask_zon
            west = pltpu.roll(east, 1, axis=1)
            h_new = h + west - east
            inv = 1.0 / h_new
            flow = jnp.maximum(east, 0.0)
            c_zon[0, l] = flow
            c_zon[1, l], c_zon[2, l] = face_terms(flow, h)
            flow = jnp.minimum(west, 0.0)
            c_zon[3, l] = flow
            c_zon[4, l], c_zon[5, l] = face_terms(flow, h)
            w_zon[0, l], w_zon[1, l] = h * inv, inv
            depth[l] = h_new
            return 0

        lax.fori_loop(0, LEV, level, 0)

    def ver_terms(s):
        flow_in = jnp.zeros((ROWS, LON), F32)
        for l in range(LEV):
            h = depth[l]
            flow = rec_b[s, l, 1] * sea
            c_ver[0, l] = flow
            if l < LEV - 1:
                c_ver[1, l], c_ver[2, l] = face_terms(flow, jnp.where(flow > 0, h, depth[l + 1]))
            inv = 1.0 / (h + flow_in - flow)
            w_ver[0, l], w_ver[1, l] = h * inv, inv
            flow_in = flow

    def wide(ref, *at):
        return jnp.broadcast_to(ref[at], (TRC, ref[at].shape[-1]))

    def flux(flow, near, far, q0, r0, l0, q1, l1, r1):
        up = flow > 0
        return (
            flow * jnp.where(up, q0, q1)
            + near * jnp.where(up, r0, l1)
            + far * jnp.where(up, l0, r1)
        )

    def columns(body):
        def column(i, _):
            body(i // 4, lanes(i % 4))
            return 0

        lax.fori_loop(0, LEV * 4, column, 0)

    def reconstruct(field, first, last):
        def body(l, y):
            q = {j: field[l, j, :, y] for j in range(first - 2, last + 2)}
            d = {f: q[f] - q[f - 1] for f in range(first - 1, last + 2)}
            e = {f: edge_dev(d[f - 1], d[f], d[f + 1]) for f in range(first, last + 1)}
            for j in range(first, last):
                dev_l[l, j, :, y], dev_r[l, j, :, y] = limited(e[j] - d[j], e[j + 1])

        columns(body)

    def meridional(field, first, last):
        def body(l, y):
            q = {j: field[l, j, :, y] for j in range(first + 2, last + 4)}
            dev = {j: (dev_l[l, j, :, y], dev_r[l, j, :, y]) for j in range(first + 2, last + 4)}
            across = {}
            for f in range(first + 3, last + 4):
                terms = [wide(c_mer, k, l, pl.ds(f - 3, 1), y) for k in range(3)]
                (l0, r0), (l1, r1) = dev[f - 1], dev[f]
                across[f] = flux(*terms, q[f - 1], r0, l0, q[f], l1, r1)
            for r in range(first, last):
                kept, inv = (wide(w_mer, k, l, pl.ds(r, 1), y) for k in range(2))
                mid[l, r, :, y] = kept * q[r + 3] + inv * (across[r + 3] - across[r + 4])

        columns(body)

    lane = lax.broadcasted_iota(jnp.int32, (TRC, BLK), 1)

    def shifted(tiles, by):
        turned = [pltpu.roll(tile, -by % BLK, axis=1) for tile in tiles]
        inside = lane < BLK - by if by > 0 else lane >= -by
        step = 1 if by > 0 else -1
        return [jnp.where(inside, turned[b], turned[(b + step) % 4]) for b in range(4)]

    def zonal_row(r):
        at = pl.ds(r, 1)
        for l in range(LEV):
            q = [mid[l, r, :, b * BLK : (b + 1) * BLK] for b in range(4)]
            west2, west, east, east2 = (shifted(q, by) for by in (-2, -1, 1, 2))
            out_east, out_west = [], []
            for b in range(4):
                d_w, d, d_e, d_ee = west[b] - west2[b], q[b] - west[b], east[b] - q[b], east2[b] - east[b]
                left, right = limited(edge_dev(d_w, d, d_e) - d, edge_dev(d, d_e, d_ee))
                v0, n0, f0, v1, n1, f1 = (wide(c_zon, k, l, at, pl.ds(b * BLK, BLK)) for k in range(6))
                out_east.append(v0 * q[b] + n0 * right + f0 * left)
                out_west.append(v1 * q[b] + n1 * left + f1 * right)
            from_west, from_east = shifted(out_east, -1), shifted(out_west, 1)
            for b in range(4):
                y = pl.ds(b * BLK, BLK)
                kept, inv = (wide(w_zon, k, l, at, y) for k in range(2))
                gain = (from_west[b] - out_east[b]) + (out_west[b] - from_east[b])
                mid2[l, :, y] = kept * q[b] + inv * gain

    def vertical_row(r, target, offset):
        def block(b, _):
            y, at = lanes(b), pl.ds(r, 1)
            q = [mid2[l, :, y] for l in range(LEV)]
            none = jnp.zeros((TRC, BLK), F32)
            d = [none] + [q[l] - q[l - 1] for l in range(1, LEV)] + [none]
            e = [none] + [edge_dev(d[f - 1], d[f], d[f + 1]) for f in range(1, LEV)] + [none]
            dev = [(none, none)] + [limited(e[l] - d[l], e[l + 1]) for l in range(1, LEV - 1)] + [(none, none)]
            across = [None]
            for f in range(1, LEV):
                terms = [wide(c_ver, k, f - 1, at, y) for k in range(3)]
                (l0, r0), (l1, r1) = dev[f - 1], dev[f]
                across.append(flux(*terms, q[f - 1], r0, l0, q[f], l1, r1))
            across.append(wide(c_ver, 0, LEV - 1, at, y) * q[LEV - 1])
            share = rate * jnp.broadcast_to(sea_f[at, y], (TRC, BLK))
            for l in range(LEV):
                kept, inv = (wide(w_ver, k, l, at, y) for k in range(2))
                gain = -across[l + 1] if l == 0 else across[l] - across[l + 1]
                new = kept * q[l] + inv * gain
                other = jnp.take_along_axis(new, partner, axis=0)
                target[l, offset + r, :, y] = new + share * (other - new)
            return 0

        lax.fori_loop(0, 4, block, 0)

    sea_f = depth.at[LEV]
    sea_f[...] = sea

    def run_rows(first, last, target, offset):
        for r in range(first, last):
            zonal_row(r)
            vertical_row(r, target, offset)

    gather_y(0)
    spread_z(2)
    gather_y(1)
    spread_z(3)
    for copy in halos:
        copy.wait_recv()
    clear_south(field_a)
    clear_north(field_a)
    reconstruct(field_a, 2, 12)
    for sem in (14, 0, 2):
        arrived(sem)
    mer_terms(0)
    meridional(field_a, 0, ROWS)
    gather_y(2)
    arrived(17)
    zon_terms(0)
    ver_terms(0)
    next_halos = field_halos(field_b, 10)
    run_rows(0, 3, field_b, 3)
    next_halos[1].start()
    gather_y(3)
    run_rows(5, 8, field_b, 3)
    next_halos[0].start()
    run_rows(3, 5, field_b, 3)

    reconstruct(field_b, 5, 9)
    for sem in (20, 1, 3):
        arrived(sem)
    mer_terms(1)
    next_halos[1].wait_recv()
    clear_north(field_b)
    reconstruct(field_b, 9, 12)
    meridional(field_b, 3, ROWS)
    arrived(23)
    zon_terms(1)
    ver_terms(1)
    stores = []

    def finish(first, last):
        run_rows(first, last, done, 0)
        part_of = pl.ds(first, last - first)
        for t in range(TRC):
            sem = local_sem.at[36 + len(stores)]
            stores.append(pltpu.make_async_copy(done.at[:, part_of, t], out.at[t, :, part_of], sem))
            stores[-1].start()

    finish(3, ROWS)
    next_halos[0].wait_recv()
    clear_south(field_b)
    reconstruct(field_b, 2, 5)
    meridional(field_b, 0, 3)
    finish(0, 3)
    for copy in halos + next_halos:
        copy.wait_send()
    for sem, like in likes.items():
        all_bytes(send_sem.at[sem], like)
    for copy in rows:
        copy.wait_send()
    for copy in stores:
        copy.wait()


def per_device(*args):
    any_space = pl.BlockSpec(memory_space=pl.ANY)
    vmem = pltpu.VMEM
    return pl.pallas_call(
        kernel,
        out_shape=jax.ShapeDtypeStruct((TRC, LEV, ROWS, LON), F32),
        in_specs=[any_space] * 7,
        out_specs=any_space,
        scratch_shapes=[
            vmem((4, RING, 2, ROWS, BLK), F32),
            *[vmem((4, 4, 2, ROWS, BLK), F32)] * 4,
            *[vmem((4, 4, 2, ROWS, BLK), F32)] * 4,
            *[vmem((4, 2, ROWS, BLK), F32)] * 4,
            *[vmem((4, 2, ROWS, BLK), F32)] * 4,
            *[vmem((LEV, ROWS, BLK), F32)] * STEPS,
            vmem((STEPS, LEV, 3, ROWS, LON), F32),
            vmem((STEPS, LEV, 2, ROWS, LON), F32),
            vmem((ROWS, LON), jnp.int32),
            vmem((ROWS, LON), jnp.int32),
            vmem((LEV, 14, TRC, LON), F32),
            vmem((LEV, 14, TRC, LON), F32),
            vmem((LEV, 14, TRC, LON), F32),
            vmem((LEV, 14, TRC, LON), F32),
            vmem((LEV, ROWS, TRC, LON), F32),
            vmem((LEV, TRC, LON), F32),
            vmem((LEV, ROWS, TRC, LON), F32),
            vmem((3, LEV, 2 * ROWS, LON), F32),
            vmem((6, LEV, ROWS, LON), F32),
            vmem((3, LEV, ROWS, LON), F32),
            vmem((2, LEV, ROWS, LON), F32),
            vmem((2, LEV, ROWS, LON), F32),
            vmem((2, LEV, ROWS, LON), F32),
            vmem((LEV + 1, ROWS, LON), F32),
            pltpu.SMEM((STEPS,), jnp.int32),
            pltpu.SMEM((TRC,), jnp.int32),
            pltpu.SMEM((TRC,), F32),
            pltpu.SemaphoreType.DMA((52,)),
            pltpu.SemaphoreType.DMA((24,)),
            pltpu.SemaphoreType.DMA((24,)),
        ],
        compiler_params=pltpu.CompilerParams(
            collective_id=0, has_side_effects=True, vmem_limit_bytes=60 * 1024 * 1024
        ),
    )(*args)


def solution(mesh):
    placed = (
        P("trc", None, "lat", None),
        P(None, "trc", None, None, "lat", None),
        P(None, "trc", None, "lat", None),
        P(),
        P("lat", None),
        P("trc"),
        P("trc"),
    )
    return jax.shard_map(
        per_device,
        mesh=mesh,
        in_specs=placed,
        out_specs=P("trc", None, "lat", None),
        check_vma=False,
    )
```

```python
import functools

import jax
import jax.numpy as jnp
from jax import lax
from jax.experimental import pallas as pl
from jax.experimental.pallas import tpu as pltpu
from jax.sharding import PartitionSpec as P

MESH = pl.DeviceIdType.MESH
TRC, LEV, ROWS, LON, STEPS, RING = 8, 4, 8, 512, 2, 16
BLK = 128
F32 = jnp.float32

GROUPS = (((0, 1), (0, -1)), ((0, 0), (0, 2)), ((1, 1), (1, -1)), ((1, 0), (1, 2)))


def limited(left, right):
    two_l, two_r = 2.0 * jnp.abs(left), 2.0 * jnp.abs(right)
    return (
        jnp.minimum(jnp.maximum(left, -two_r), two_r),
        jnp.minimum(jnp.maximum(right, -two_l), two_l),
    )


def edge_dev(before, here, after):
    dev = 0.5 * here + (1.0 / 12.0) * (before - after)
    return jnp.minimum(jnp.maximum(dev, jnp.minimum(here, 0.0)), jnp.maximum(here, 0.0))


def face_terms(flow, depth_up):
    courant = jnp.abs(flow) / jnp.maximum(depth_up, 0.25)
    rest = 1.0 - courant
    scaled = flow * rest
    return scaled * rest, -courant * scaled


def kernel(
    tracers, transports, thickness, owner, land_sea, pairs, rates, out,
    stage, along_y0, along_y1, along_y2, along_y3, along_z0, along_z1, along_z2, along_z3,
    quarter0, quarter1, quarter2, quarter3, part0, part1, part2, part3, border0, border1, rec_a, rec_b, sea_int, sea_halo_int,
    field_a, field_b, dev_l, dev_r, mid, mid2, done,
    c_mer, c_zon, c_ver, w_mer, w_zon, w_ver, depth,
    owner_s, pairs_s, rates_s,
    local_sem, send_sem, recv_sem,
):
    along_y, along_z = (along_y0, along_y1, along_y2, along_y3), (along_z0, along_z1, along_z2, along_z3)
    quarter, part = (quarter0, quarter1, quarter2, quarter3), (part0, part1, part2, part3)
    border = (border0, None, border1)
    lat, me = lax.axis_index("lat"), lax.axis_index("trc")
    my_y, my_z = me // 4, me % 4
    north, south = lax.rem(lat + 1, RING), lax.rem(lat + RING - 1, RING)

    def lanes(y):
        return pl.ds(pl.multiple_of(y * BLK, BLK), BLK)

    barrier = pltpu.get_barrier_semaphore()

    for beside in (north, south):
        pl.semaphore_signal(barrier, inc=1, device_id={"lat": beside}, device_id_type=MESH)
    for k in range(1, 4):
        for peer in (my_y * 4 + lax.rem(my_z + k, 4), lax.rem(my_y + k, 4) * 4 + my_z):
            pl.semaphore_signal(barrier, inc=1, device_id={"trc": peer}, device_id_type=MESH)

    stages = []
    for g, fields in enumerate(GROUPS):
        copies = []
        for f, (s, k) in enumerate(fields):
            source = thickness.at[s, 0] if k < 0 else transports.at[s, 0, k]
            for y in range(4):
                copies.append(
                    pltpu.make_async_copy(
                        source.at[:, :, pl.ds(y * BLK, BLK)],
                        stage.at[g, pl.ds(4 * y, 4), f],
                        local_sem.at[8 * g + 4 * f + y],
                    )
                )
        for copy in copies:
            copy.start()
        stages.append(copies)
    smalls = [
        pltpu.make_async_copy(owner, owner_s, local_sem.at[32]),
        pltpu.make_async_copy(pairs, pairs_s, local_sem.at[33]),
        pltpu.make_async_copy(rates, rates_s, local_sem.at[34]),
        pltpu.make_async_copy(land_sea, sea_int, local_sem.at[35]),
    ]
    loads = [
        pltpu.make_async_copy(
            tracers.at[t], field_a.at[:, pl.ds(3, ROWS), t], local_sem.at[36 + t]
        )
        for t in range(TRC)
    ]
    for copy in smalls + loads:
        copy.start()

    pl.semaphore_wait(barrier, 8)

    def one_copy(source, target, sem, **where):
        return pltpu.make_async_remote_copy(
            source, target, send_sem.at[sem], recv_sem.at[sem], device_id=where, device_id_type=MESH
        )

    def along(axis, source, target, sem):
        for k in (2, 1, 3):
            if axis == "y":
                at = lax.rem(my_y + k, 4)
                one_copy(source(at), target, sem, trc=at * 4 + my_z).start()
            else:
                at = lax.rem(my_z + k, 4)
                one_copy(source(at), target, sem, trc=my_y * 4 + at).start()

    def all_bytes(sems, like):
        pltpu.make_async_copy(like, like, sems).wait()

    for_north, for_south = pl.ds(0, 1), pl.ds(1, 2)

    def put_border(rows, tile):
        rows[0:1], rows[1:2], rows[2:3] = tile[1, 7:8], tile[1, 0:1], tile[0, 0:1]

    three = pl.ds(0, 3)
    likes = {s + 2 * i: rec_a.at[s, :, 2, rows] for s in range(STEPS) for i, rows in enumerate((for_north, for_south))}
    for g in range(4):
        for k in range(3):
            likes[12 + 3 * g + k] = along_y[g].at[three]

    def arrived(sem):
        all_bytes(recv_sem.at[sem], likes[sem])

    def scatter_y(g):
        for copy in stages[g]:
            copy.wait()
        along("y", lambda y: stage.at[g, pl.ds(4 * y, 4)], along_y[g].at[my_y], 12 + 3 * g)
        along_y[g][my_y] = stage[g, pl.ds(4 * my_y, 4)]

    def spread_z(g):
        arrived(12 + 3 * g)
        quarter[g][...] = along_y[g][owner_s[g // 2] // 4]
        along("z", lambda z: quarter[g], along_z[g].at[my_z], 13 + 3 * g)
        along_z[g][my_z] = quarter[g][...]

    def gather_y(g):
        arrived(13 + 3 * g)
        part[g][...] = along_z[g][lax.rem(owner_s[g // 2], 4)]
        s, first = g // 2, g % 2 == 0
        rec = (rec_a if first else rec_b).at[s, :, pl.ds(0, 2), :, lanes(my_y)]
        along("y", lambda y: part[g], rec, 14 + 3 * g)
        if first:
            for l in range(LEV):
                put_border(border[g].at[l], part[g][l])
            for k in (2, 1, 3, 0):
                there = lax.rem(my_y + k, 4) * 4 + my_z
                for part_of, sem, where in ((for_north, s, north), (for_south, s + 2, south)):
                    target = rec_a.at[s, :, 2, part_of, lanes(my_y)]
                    one_copy(border[g].at[:, part_of], target, sem, lat=where, trc=there).start()
        rec[...] = part[g][...]

    def field_halos(field, sem):
        return [
            one_copy(field.at[:, pl.ds(8, 3)], field.at[:, pl.ds(0, 3)], sem, lat=north),
            one_copy(field.at[:, pl.ds(3, 3)], field.at[:, pl.ds(11, 3)], sem + 1, lat=south),
        ]

    def clear_south(field):
        @pl.when(lat == 0)
        def _():
            field[:, 0:3] = jnp.zeros((LEV, 3, TRC, LON), F32)

    def clear_north(field):
        @pl.when(lat == RING - 1)
        def _():
            field[:, 11:14] = jnp.zeros((LEV, 3, TRC, LON), F32)

    for copy in loads:
        copy.wait()
    halos = field_halos(field_a, 8)
    for copy in halos:
        copy.start()

    for g in range(2):
        scatter_y(g)
    rows = [
        one_copy(land_sea.at[pl.ds(7, 1)], sea_halo_int.at[pl.ds(0, 1)], 6, lat=north),
        one_copy(land_sea.at[pl.ds(0, 1)], sea_halo_int.at[pl.ds(1, 1)], 7, lat=south),
    ]
    for copy in rows:
        copy.start()
    for copy in smalls:
        copy.wait()
    spread_z(0)
    scatter_y(2)
    spread_z(1)
    scatter_y(3)


    for copy in rows:
        copy.wait_recv()
    sub = lax.broadcasted_iota(jnp.int32, (ROWS, LON), 0)
    sea = sea_int[...].astype(F32)
    sea_s = jnp.where(lat > 0, sea_halo_int[0:1].astype(F32), 0.0)
    sea_n = jnp.where(lat < RING - 1, sea_halo_int[1:2].astype(F32), 0.0)
    mask_mer = sea * jnp.where(sub == 0, sea_s, pltpu.roll(sea, 1, axis=0))
    mask_top = sea[7:8] * sea_n
    mask_zon = sea * pltpu.roll(sea, LON - 1, axis=1)
    sub1 = lax.broadcasted_iota(jnp.int32, (TRC, BLK), 0)
    partner = jnp.zeros((TRC, BLK), jnp.int32)
    rate = jnp.zeros((TRC, BLK), F32)
    for i in range(TRC):
        partner = jnp.where(sub1 == i, pairs_s[i] - me * TRC, partner)
        rate = jnp.where(sub1 == i, rates_s[i], rate)

    def mer_terms(s):
        def level(l, _):
            flow0, h, x = rec_a[s, l, 0], rec_a[s, l, 1], rec_a[s, l, 2]
            flow = flow0 * mask_mer
            below = jnp.where(sub == 0, x[0:1], pltpu.roll(h, 1, axis=0))
            near, far = face_terms(flow, jnp.where(flow > 0, below, h))
            c_mer[0, l, 0:8], c_mer[1, l, 0:8], c_mer[2, l, 0:8] = flow, near, far
            top = x[2:3] * mask_top
            near, far = face_terms(top, jnp.where(top > 0, h[7:8], x[1:2]))
            c_mer[0, l, 8:9], c_mer[1, l, 8:9], c_mer[2, l, 8:9] = top, near, far
            h_new = h + flow - jnp.where(sub == 7, top, pltpu.roll(flow, 7, axis=0))
            inv = 1.0 / h_new
            w_mer[0, l], w_mer[1, l] = h * inv, inv
            depth[l] = h_new
            return 0

        lax.fori_loop(0, LEV, level, 0)

    def zon_terms(s):
        def level(l, _):
            h = depth[l]
            east = rec_b[s, l, 0] * mask_zon
            west = pltpu.roll(east, 1, axis=1)
            h_new = h + west - east
            inv = 1.0 / h_new
            flow = jnp.maximum(east, 0.0)
            c_zon[0, l] = flow
            c_zon[1, l], c_zon[2, l] = face_terms(flow, h)
            flow = jnp.minimum(west, 0.0)
            c_zon[3, l] = flow
            c_zon[4, l], c_zon[5, l] = face_terms(flow, h)
            w_zon[0, l], w_zon[1, l] = h * inv, inv
            depth[l] = h_new
            return 0

        lax.fori_loop(0, LEV, level, 0)

    def ver_terms(s):
        flow_in = jnp.zeros((ROWS, LON), F32)
        for l in range(LEV):
            h = depth[l]
            flow = rec_b[s, l, 1] * sea
            c_ver[0, l] = flow
            if l < LEV - 1:
                c_ver[1, l], c_ver[2, l] = face_terms(flow, jnp.where(flow > 0, h, depth[l + 1]))
            inv = 1.0 / (h + flow_in - flow)
            w_ver[0, l], w_ver[1, l] = h * inv, inv
            flow_in = flow

    def wide(ref, *at):
        return jnp.broadcast_to(ref[at], (TRC, ref[at].shape[-1]))

    def flux(flow, near, far, q0, r0, l0, q1, l1, r1):
        up = flow > 0
        return (
            flow * jnp.where(up, q0, q1)
            + near * jnp.where(up, r0, l1)
            + far * jnp.where(up, l0, r1)
        )

    def columns(body):
        def column(i, _):
            body(i // 4, lanes(i % 4))
            return 0

        lax.fori_loop(0, LEV * 4, column, 0)

    def reconstruct(field, first, last):
        def body(l, y):
            q = {j: field[l, j, :, y] for j in range(first - 2, last + 2)}
            d = {f: q[f] - q[f - 1] for f in range(first - 1, last + 2)}
            e = {f: edge_dev(d[f - 1], d[f], d[f + 1]) for f in range(first, last + 1)}
            for j in range(first, last):
                dev_l[l, j, :, y], dev_r[l, j, :, y] = limited(e[j] - d[j], e[j + 1])

        columns(body)

    def meridional(field, first, last):
        def body(l, y):
            q = {j: field[l, j, :, y] for j in range(first + 2, last + 4)}
            dev = {j: (dev_l[l, j, :, y], dev_r[l, j, :, y]) for j in range(first + 2, last + 4)}
            across = {}
            for f in range(first + 3, last + 4):
                terms = [wide(c_mer, k, l, pl.ds(f - 3, 1), y) for k in range(3)]
                (l0, r0), (l1, r1) = dev[f - 1], dev[f]
                across[f] = flux(*terms, q[f - 1], r0, l0, q[f], l1, r1)
            for r in range(first, last):
                kept, inv = (wide(w_mer, k, l, pl.ds(r, 1), y) for k in range(2))
                mid[l, r, :, y] = kept * q[r + 3] + inv * (across[r + 3] - across[r + 4])

        columns(body)

    lane = lax.broadcasted_iota(jnp.int32, (TRC, BLK), 1)

    def shifted(tiles, by):
        turned = [pltpu.roll(tile, -by % BLK, axis=1) for tile in tiles]
        inside = lane < BLK - by if by > 0 else lane >= -by
        step = 1 if by > 0 else -1
        return [jnp.where(inside, turned[b], turned[(b + step) % 4]) for b in range(4)]

    def zonal_row(r):
        at = pl.ds(r, 1)
        for l in range(LEV):
            q = [mid[l, r, :, b * BLK : (b + 1) * BLK] for b in range(4)]
            west2, west, east, east2 = (shifted(q, by) for by in (-2, -1, 1, 2))
            out_east, out_west = [], []
            for b in range(4):
                d_w, d, d_e, d_ee = west[b] - west2[b], q[b] - west[b], east[b] - q[b], east2[b] - east[b]
                left, right = limited(edge_dev(d_w, d, d_e) - d, edge_dev(d, d_e, d_ee))
                v0, n0, f0, v1, n1, f1 = (wide(c_zon, k, l, at, pl.ds(b * BLK, BLK)) for k in range(6))
                out_east.append(v0 * q[b] + n0 * right + f0 * left)
                out_west.append(v1 * q[b] + n1 * left + f1 * right)
            from_west, from_east = shifted(out_east, -1), shifted(out_west, 1)
            for b in range(4):
                y = pl.ds(b * BLK, BLK)
                kept, inv = (wide(w_zon, k, l, at, y) for k in range(2))
                gain = (from_west[b] - out_east[b]) + (out_west[b] - from_east[b])
                mid2[l, :, y] = kept * q[b] + inv * gain

    def vertical_row(r, target, offset):
        def block(b, _):
            y, at = lanes(b), pl.ds(r, 1)
            q = [mid2[l, :, y] for l in range(LEV)]
            none = jnp.zeros((TRC, BLK), F32)
            d = [none] + [q[l] - q[l - 1] for l in range(1, LEV)] + [none]
            e = [none] + [edge_dev(d[f - 1], d[f], d[f + 1]) for f in range(1, LEV)] + [none]
            dev = [(none, none)] + [limited(e[l] - d[l], e[l + 1]) for l in range(1, LEV - 1)] + [(none, none)]
            across = [None]
            for f in range(1, LEV):
                terms = [wide(c_ver, k, f - 1, at, y) for k in range(3)]
                (l0, r0), (l1, r1) = dev[f - 1], dev[f]
                across.append(flux(*terms, q[f - 1], r0, l0, q[f], l1, r1))
            across.append(wide(c_ver, 0, LEV - 1, at, y) * q[LEV - 1])
            share = rate * jnp.broadcast_to(sea_f[at, y], (TRC, BLK))
            for l in range(LEV):
                kept, inv = (wide(w_ver, k, l, at, y) for k in range(2))
                gain = -across[l + 1] if l == 0 else across[l] - across[l + 1]
                new = kept * q[l] + inv * gain
                other = jnp.take_along_axis(new, partner, axis=0)
                target[l, offset + r, :, y] = new + share * (other - new)
            return 0

        lax.fori_loop(0, 4, block, 0)

    sea_f = depth.at[LEV]
    sea_f[...] = sea

    def run_rows(first, last, target, offset):
        for r in range(first, last):
            zonal_row(r)
            vertical_row(r, target, offset)

    gather_y(0)
    spread_z(2)
    gather_y(1)
    for copy in halos:
        copy.wait_recv()
    clear_south(field_a)
    clear_north(field_a)
    reconstruct(field_a, 2, 12)
    for sem in (14, 0, 2):
        arrived(sem)
    spread_z(3)
    mer_terms(0)
    meridional(field_a, 0, ROWS)
    gather_y(2)
    arrived(17)
    zon_terms(0)
    ver_terms(0)
    next_halos = field_halos(field_b, 10)
    run_rows(0, 3, field_b, 3)
    next_halos[1].start()
    gather_y(3)
    run_rows(5, 8, field_b, 3)
    next_halos[0].start()
    run_rows(3, 5, field_b, 3)

    reconstruct(field_b, 5, 9)
    for sem in (20, 1, 3):
        arrived(sem)
    mer_terms(1)
    next_halos[1].wait_recv()
    clear_north(field_b)
    reconstruct(field_b, 9, 12)
    meridional(field_b, 3, ROWS)
    arrived(23)
    zon_terms(1)
    ver_terms(1)
    stores = []

    def finish(first, last):
        run_rows(first, last, done, 0)
        part_of = pl.ds(first, last - first)
        for t in range(TRC):
            sem = local_sem.at[36 + len(stores)]
            stores.append(pltpu.make_async_copy(done.at[:, part_of, t], out.at[t, :, part_of], sem))
            stores[-1].start()

    finish(3, ROWS)
    next_halos[0].wait_recv()
    clear_south(field_b)
    reconstruct(field_b, 2, 5)
    meridional(field_b, 0, 3)
    finish(0, 3)
    for copy in halos + next_halos:
        copy.wait_send()
    for sem, like in likes.items():
        all_bytes(send_sem.at[sem], like)
    for copy in rows:
        copy.wait_send()
    for copy in stores:
        copy.wait()


def per_device(*args):
    any_space = pl.BlockSpec(memory_space=pl.ANY)
    vmem = pltpu.VMEM
    return pl.pallas_call(
        kernel,
        out_shape=jax.ShapeDtypeStruct((TRC, LEV, ROWS, LON), F32),
        in_specs=[any_space] * 7,
        out_specs=any_space,
        scratch_shapes=[
            vmem((4, RING, 2, ROWS, BLK), F32),
            *[vmem((4, 4, 2, ROWS, BLK), F32)] * 4,
            *[vmem((4, 4, 2, ROWS, BLK), F32)] * 4,
            *[vmem((4, 2, ROWS, BLK), F32)] * 4,
            *[vmem((4, 2, ROWS, BLK), F32)] * 4,
            *[vmem((LEV, ROWS, BLK), F32)] * STEPS,
            vmem((STEPS, LEV, 3, ROWS, LON), F32),
            vmem((STEPS, LEV, 2, ROWS, LON), F32),
            vmem((ROWS, LON), jnp.int32),
            vmem((ROWS, LON), jnp.int32),
            vmem((LEV, 14, TRC, LON), F32),
            vmem((LEV, 14, TRC, LON), F32),
            vmem((LEV, 14, TRC, LON), F32),
            vmem((LEV, 14, TRC, LON), F32),
            vmem((LEV, ROWS, TRC, LON), F32),
            vmem((LEV, TRC, LON), F32),
            vmem((LEV, ROWS, TRC, LON), F32),
            vmem((3, LEV, 2 * ROWS, LON), F32),
            vmem((6, LEV, ROWS, LON), F32),
            vmem((3, LEV, ROWS, LON), F32),
            vmem((2, LEV, ROWS, LON), F32),
            vmem((2, LEV, ROWS, LON), F32),
            vmem((2, LEV, ROWS, LON), F32),
            vmem((LEV + 1, ROWS, LON), F32),
            pltpu.SMEM((STEPS,), jnp.int32),
            pltpu.SMEM((TRC,), jnp.int32),
            pltpu.SMEM((TRC,), F32),
            pltpu.SemaphoreType.DMA((52,)),
            pltpu.SemaphoreType.DMA((24,)),
            pltpu.SemaphoreType.DMA((24,)),
        ],
        compiler_params=pltpu.CompilerParams(
            collective_id=0, has_side_effects=True, vmem_limit_bytes=60 * 1024 * 1024
        ),
    )(*args)


def solution(mesh):
    placed = (
        P("trc", None, "lat", None),
        P(None, "trc", None, None, "lat", None),
        P(None, "trc", None, "lat", None),
        P(),
        P("lat", None),
        P("trc"),
        P("trc"),
    )
    return jax.shard_map(
        per_device,
        mesh=mesh,
        in_specs=placed,
        out_specs=P("trc", None, "lat", None),
        check_vma=False,
    )
```
